256 devices in a mesh: dp: 16 (over x, y), seq: 16 (over z, core).
Axes of the slice: x: 4, y: 4, z: 8, core: 2. Of those that a mesh axis runs over, the one named last changes fastest.
Arguments:
- tokens: bfloat16 [16, 2048, 1024], P('dp', 'seq'), may hold values from -6 to 6
- cotangent: bfloat16 [16, 2048, 1024], P('dp', 'seq'), may hold values from -6 to 6
- w_in: bfloat16 [2048, 1024], replicated, may hold values from -0.1875 to 0.1875
- w_out: bfloat16 [512, 1024], replicated, may hold values from -0.25 to 0.25
- input_norm_gain: float32 [1024], replicated, may hold values from 0.25 to 1.75
- gain_out: float32 [512], replicated, may hold values from 0.25 to 1.75
- time_bias: float32 [128, 4], replicated, may hold values from -4 to 4
- lengths: int32 [16], P('dp'), may hold values from 1 to 2048, as said below
- assignment: int32 [16, 16], P('dp'), may hold values from 0 to 15, each once within a row
- buckets: int32 [16, 16, 16], P('dp'), may hold values from 0 to 127
- block_mask: int32 [16, 16, 16], P('dp'), may hold values 0 or 1
Outputs:
- mixed: bfloat16 [16, 2048, 1024], P('dp', 'seq')
- grad_tokens: bfloat16 [16, 2048, 1024], P('dp', 'seq')
- grad_in: float32 [2048, 1024], P(('dp', 'seq'))
- grad_out: float32 [512, 1024], P(('dp', 'seq'))
The draws below stay inside these ranges and needn't reach their ends.
Inputs may be any that keep to these rules, and one draw needn't show every extreme that they name: `lengths`: each group holds one history; some group's history fills all 2048 slots.
All inputs are finite; a program needn't handle non-finite values. No bound on the sum of `block_mask` on one device may be relied on, other than what follows from the above.
Results may differ from the reference program's by a relative error of at most 0.017.
Values may be sent and summed in bfloat16 or wider, within the bound.
No kernel may reach another device: no remote copies, remote signals or barrier semaphores. Data moves between devices by JAX's collectives and lax.ppermute only.
A program may use at most 64 MiB of HBM per device.

```python
import math
import jax
import jax.numpy as jnp
from jax import lax

D = 1024
HEADS = 4
DH = 128
BUCKETS = 128
BLOCK = 128
SLOTS = 2048
HD = 512
N_DP = 16
N_SEQ = 16


def draw_lengths(key, part):
    key = jax.random.fold_in(key, 11)
    first, second = jax.random.split(key)
    values = jax.random.randint(first, (N_DP,), 1, SLOTS + 1)
    longest = jax.random.randint(second, (), 0, N_DP)
    return jnp.where(jnp.arange(N_DP) == longest, SLOTS, values).astype(jnp.int32)


def with_ends(values, rng, least, high):
    extent = values.shape
    spot = [jax.random.randint(jax.random.fold_in(rng, axis), (), 0, extent[axis]) for axis in range(len(extent))]
    values = values.at[tuple(spot)].set(least)
    longest = extent.index(max(extent))
    spot[longest] = (spot[longest] + 1) % extent[longest]
    return values.at[tuple(spot)].set(high)


def shard_levels(own_key, extent, pieces, smallest, top_value):
    def one(dim, parts):
        steps = jax.random.uniform(jax.random.fold_in(jax.random.fold_in(own_key, 6), dim), (parts,), jnp.float32, smallest / len(pieces), top_value / len(pieces))
        return jnp.repeat(jnp.exp(steps), extent[dim] // parts).reshape((-1,) + (1,) * (len(extent) - dim - 1))

    loudness = one(*pieces[0])
    for cut in pieces[1:]:
        loudness = loudness * one(*cut)
    return loudness


def bell_draw(own_key, dims, spread, reach, cuts=(), kind=jnp.bfloat16):
    entries = spread * jax.random.normal(own_key, dims, jnp.float32)
    if cuts:
        entries = entries * shard_levels(own_key, dims, cuts, -0.22, 0.18)
    return jnp.clip(entries, -reach, reach).astype(kind)


def setup_inputs(seed: int = 0) -> dict:
    arg_keys = jax.random.split(jax.random.key(seed), 12)
    tokens = bell_draw(arg_keys[0], (N_DP, SLOTS, D), 1.0, 6.0, ((0, 16), (1, 16)))
    cotangent = bell_draw(arg_keys[1], (N_DP, SLOTS, D), 1.0, 6.0, ((0, 16), (1, 16)))
    w_in = bell_draw(arg_keys[2], (4 * HD, D), D ** -0.5, 0.1875)
    w_out = bell_draw(arg_keys[3], (HD, D), HD ** -0.5, 0.25)
    input_norm_gain = jnp.clip(1.0 + 0.15 * jax.random.normal(arg_keys[4], (D,), jnp.float32), 0.25, 1.75)
    gain_out = jnp.clip(1.0 + 0.15 * jax.random.normal(arg_keys[5], (HD,), jnp.float32), 0.25, 1.75)
    time_bias = bell_draw(arg_keys[6], (BUCKETS, HEADS), 1.0, 4.0, (), jnp.float32)
    lengths = draw_lengths(jax.random.fold_in(arg_keys[11], 71), 0)
    assignment = jax.vmap(lambda own: jax.random.permutation(own, N_SEQ))(jax.random.split(arg_keys[8], N_DP)).reshape((N_DP, N_SEQ)).astype(jnp.int32)
    buckets = with_ends(jax.random.randint(arg_keys[9], (N_DP, N_SEQ, N_SEQ), 0, BUCKETS), jax.random.fold_in(arg_keys[9], 1), 0, BUCKETS - 1).astype(jnp.int32)
    block_mask = with_ends((jax.random.randint(arg_keys[10], (N_DP, N_SEQ, N_SEQ), 0, 4) < 3).astype(jnp.int32), jax.random.fold_in(arg_keys[10], 1), 0, 1)
    return {"tokens": tokens, "cotangent": cotangent, "w_in": w_in, "w_out": w_out, "input_norm_gain": input_norm_gain, "gain_out": gain_out, "time_bias": time_bias, "lengths": lengths, "assignment": assignment, "buckets": buckets, "block_mask": block_mask}


EPS = 1e-05

def silu_slope(values):
    sig = jax.nn.sigmoid(values)
    return sig * (1.0 + values * (1.0 - sig))

def normalize_rows(values):
    mean = lax.optimization_barrier(jnp.mean(values, -1, keepdims=True))
    centred = values - mean
    var = lax.optimization_barrier(jnp.mean(centred * centred, -1, keepdims=True))
    rstd = lax.rsqrt(var + EPS)
    return (centred * rstd, rstd)

def norm_backward_pass(grad_hat, hat, rstd):
    first = lax.optimization_barrier(jnp.mean(grad_hat, -1, keepdims=True))
    second = lax.optimization_barrier(jnp.mean(grad_hat * hat, -1, keepdims=True))
    return rstd * (grad_hat - first - hat * second)

def expand_pairs(values):
    return jnp.repeat(jnp.repeat(values, BLOCK, 0), BLOCK, 1)

def reference(tokens, cotangent, w_in, w_out, input_norm_gain, gain_out, time_bias, lengths, assignment, buckets, block_mask):
    alpha = 1.0 / math.sqrt(DH)
    width = HEADS * DH
    grad_scale = 1.0 / math.sqrt(N_DP * SLOTS)

    def to_heads(rows):
        return rows.reshape(SLOTS, HEADS, DH).transpose(1, 0, 2)

    def group_pass(carry, inputs):
        sum_in, sum_out = carry
        x, output_gradient_rows, length, table, bucket_g, mask_g = inputs
        lenf = length.astype(jnp.float32)
        input_float_rows = x.astype(jnp.float32)
        standardized_input, inverse_input_norm = normalize_rows(input_float_rows)
        normalized_rows = (standardized_input * input_norm_gain).astype(jnp.bfloat16)
        pre = jnp.dot(normalized_rows, w_in.T, preferred_element_type=jnp.float32)
        proj = jax.nn.silu(pre).astype(jnp.bfloat16)
        u = proj[:, :width]
        v = proj[:, width:2 * width]
        q = proj[:, 2 * width:3 * width]
        k = proj[:, 3 * width:]
        pos = (jnp.repeat(table, BLOCK) * BLOCK + jnp.tile(jnp.arange(BLOCK, dtype=jnp.int32), N_SEQ)).astype(jnp.int32)
        pair_bucket = bucket_g[table[:, None], table[None, :]]
        pair_mask = mask_g[table[:, None], table[None, :]]
        live = (pos[None, :] <= pos[:, None]) & (pos[:, None] < length) & (pos[None, :] < length) & (expand_pairs(pair_mask) > 0)
        bias_pairs = jnp.moveaxis(time_bias[pair_bucket], -1, 0)

        def head_scores(qh, kh, bias_h):
            return jnp.dot(qh, kh.T, preferred_element_type=jnp.float32) * alpha + expand_pairs(bias_h)

        def head_forward(args):
            qh, kh, vh, bias_h = args
            scores = head_scores(qh, kh, bias_h)
            weights = jnp.where(live, jax.nn.silu(scores) / lenf, 0.0).astype(jnp.bfloat16)
            return jnp.dot(weights, vh, preferred_element_type=jnp.float32)
        q_t, k_t, v_t = (to_heads(q), to_heads(k), to_heads(v))
        attn = lax.map(head_forward, (q_t, k_t, v_t, bias_pairs))
        attn = attn.transpose(1, 0, 2).reshape(SLOTS, width)
        ohat, rout = normalize_rows(attn)
        z = (ohat * gain_out * u.astype(jnp.float32)).astype(jnp.bfloat16)
        mixed = (input_float_rows + jnp.dot(z, w_out, preferred_element_type=jnp.float32)).astype(jnp.bfloat16)
        dz = jnp.dot(output_gradient_rows, w_out.T, preferred_element_type=jnp.float32)
        du = dz * ohat * gain_out
        dnh = dz * gain_out * u.astype(jnp.float32)
        dattn = norm_backward_pass(dnh, ohat, rout).astype(jnp.bfloat16)

        def head_backward(args):
            qh, kh, vh, bias_h, doh = args
            scores = head_scores(qh, kh, bias_h)
            weights = jnp.where(live, jax.nn.silu(scores) / lenf, 0.0).astype(jnp.bfloat16)
            grad_a = jnp.dot(doh, vh.T, preferred_element_type=jnp.float32)
            grad_s = jnp.where(live, grad_a * silu_slope(scores) / lenf, 0.0).astype(jnp.bfloat16)
            dq = jnp.dot(grad_s, kh, preferred_element_type=jnp.float32) * alpha
            dk = jnp.dot(grad_s.T, qh, preferred_element_type=jnp.float32) * alpha
            dv = jnp.dot(weights.T, doh, preferred_element_type=jnp.float32)
            return (dq, dk, dv)
        dq, dk, dv = lax.map(head_backward, (q_t, k_t, v_t, bias_pairs, to_heads(dattn)))

        def join(values):
            return values.transpose(1, 0, 2).reshape(SLOTS, width)
        dproj = jnp.concatenate([du, join(dv), join(dq), join(dk)], axis=1)
        dpre = (dproj * silu_slope(pre)).astype(jnp.bfloat16)
        term_in = jnp.dot(dpre.T, normalized_rows, preferred_element_type=jnp.float32)
        term_out = jnp.dot(z.T, output_gradient_rows, preferred_element_type=jnp.float32)
        normed_input_gradient = jnp.dot(dpre, w_in, preferred_element_type=jnp.float32) * input_norm_gain
        input_gradient = (output_gradient_rows.astype(jnp.float32) + norm_backward_pass(normed_input_gradient, standardized_input, inverse_input_norm)).astype(jnp.bfloat16)
        return ((sum_in + term_in, sum_out + term_out), (mixed, input_gradient))
    start = (jnp.zeros((4 * width, D), jnp.float32), jnp.zeros((width, D), jnp.float32))
    sums, outs = lax.scan(group_pass, start, (tokens, cotangent, lengths, assignment, buckets, block_mask))
    return (outs[0], outs[1], sums[0] * grad_scale, sums[1] * grad_scale)
```

```python
import functools
import math

import jax
import jax.numpy as jnp
from jax import lax
from jax.experimental import pallas as pl
from jax.experimental.pallas import tpu as pltpu
from jax.sharding import PartitionSpec as P

EPS = 1e-05
SEQ = 16
GROUPS = 16
ROWS = 128
HEADS = 4
DH = 128
WIDTH = HEADS * DH
MODEL = 1024
ALPHA = 1.0 / math.sqrt(DH)
GRAD_SCALE = 1.0 / math.sqrt(SEQ * GROUPS * ROWS)
FAR = 1 << 20
ZROWS = WIDTH // GROUPS
CHUNK = ROWS + ZROWS
NT = (((1,), (1,)), ((), ()))
SMEM = pl.BlockSpec(memory_space=pltpu.SMEM)
VMEM = pl.BlockSpec(memory_space=pltpu.VMEM)
F32 = jnp.float32
BF16 = jnp.bfloat16

STEPS = ((0, 2), (2, 4), (6, 4), (10, 4), (14, 2))


def nt_dot(a, b):
    return lax.dot_general(a, b, NT, preferred_element_type=F32)


def nn_dot(a, b):
    return jnp.dot(a, b, preferred_element_type=F32)


def silu(values):
    half = 0.5 * values
    return half * (jnp.tanh(half) + 1.0)


def silu_slope(values):
    half = 0.5 * values
    turn = jnp.tanh(half)
    return 0.5 * (1.0 + turn) * (1.0 + half * (1.0 - turn))


def normalize_rows(values):
    mean = jnp.mean(values, -1, keepdims=True)
    centred = values - mean
    var = jnp.mean(centred * centred, -1, keepdims=True)
    rstd = lax.rsqrt(var + EPS)
    return (centred * rstd, rstd)


def norm_backward(grad_hat, hat, rstd):
    first = jnp.mean(grad_hat, -1, keepdims=True)
    second = jnp.mean(grad_hat * hat, -1, keepdims=True)
    return rstd * (grad_hat - first - hat * second)


def cols(head):
    return slice(head * DH, (head + 1) * DH)


def part(index):
    return slice(index * ROWS, (index + 1) * ROWS)


def weight_spec(index):
    return pl.BlockSpec((WIDTH, MODEL), lambda i: (index, 0))


def call(kernel, out_shape, in_specs, out_specs=None, scratch=(), flops=0, moved=0, limit=40, **kw):
    if out_specs is None:
        out_specs = jax.tree.map(lambda _: VMEM, out_shape)
    return pl.pallas_call(
        kernel,
        out_shape=out_shape,
        grid=(1,),
        in_specs=in_specs,
        out_specs=out_specs,
        scratch_shapes=list(scratch),
        compiler_params=pltpu.CompilerParams(vmem_limit_bytes=limit << 20),
        cost_estimate=pl.CostEstimate(flops=flops, bytes_accessed=moved, transcendentals=0),
        **kw,
    )


def shape(*dims, dtype=F32):
    return jax.ShapeDtypeStruct(dims, dtype)


def slot_of(me, place):
    if place < 2:
        return me ^ place
    step, rest = divmod(place - 2, 4)
    shift = 2 * (step + 1)
    base = (me - shift + SEQ) if rest < 2 else (me + shift)
    return (base & (SEQ - 1)) ^ (rest & 1)


def scalars_kernel(me_ref, length_ref, table_ref, bucket_ref, mask_ref, bias_ref, ints, floats):
    me = me_ref[0]
    length = length_ref[0]
    own = table_ref[0, me]
    for place in range(SEQ):
        block = table_ref[0, slot_of(me, place)]
        ints[place] = jnp.where(mask_ref[0, own, block] > 0, (own - block) * ROWS, -FAR)
        ints[SEQ + place] = jnp.where(mask_ref[0, block, own] > 0, (block - own) * ROWS, -FAR)
        ints[2 * SEQ + place] = length - block * ROWS
        query_bucket = bucket_ref[0, own, block]
        key_bucket = bucket_ref[0, block, own]
        for head in range(HEADS):
            floats[place * HEADS + head] = 0.5 * bias_ref[query_bucket, head]
            floats[(SEQ + place) * HEADS + head] = 0.5 * bias_ref[key_bucket, head]
    ints[3 * SEQ] = length - own * ROWS
    floats[2 * SEQ * HEADS] = 1.0 / jnp.full((), length, F32)


def make_scalars(me, lengths, assignment, buckets, block_mask, time_bias):
    return call(
        scalars_kernel,
        (shape(64, dtype=jnp.int32), shape(256)),
        [SMEM] * 6,
        (SMEM, SMEM),
    )(me, lengths, assignment, buckets, block_mask, time_bias)


def query_gap(ints):
    row = lax.broadcasted_iota(jnp.int32, (ROWS, ROWS), 0)
    col = lax.broadcasted_iota(jnp.int32, (ROWS, ROWS), 1)
    return jnp.where(row < ints[3 * SEQ], col - row, FAR)


def own_kernel(x_ref, cot_ref, w_in, w_out, gain, pre_ref, dz_ref, both_ref):
    hat, _ = normalize_rows(x_ref[...].astype(F32))
    normed = (hat * gain[...]).astype(BF16)
    both_ref[0] = normed
    both_ref[1] = cot_ref[...]
    pre_ref[...] = nt_dot(normed, w_in[...])
    dz_ref[...] = nt_dot(cot_ref[...], w_out[...])


def forward_kernel(count, first, last, *refs):
    refs = list(refs)
    take = lambda n: [refs.pop(0) for _ in range(n)]
    ints, floats = take(2)
    toks = take(count)
    w_v, w_q, w_k, gain = take(4)
    own_q = attn_in = None
    if first:
        own_q, attn_in = take(2)
    if last:
        pre_ref, dz_ref, gain_out = take(3)
    k_ref, v_ref, q_ref = take(3)
    if last:
        dattn_ref, ohat_ref = take(2)
    else:
        (attn_ref,) = take(1)
    (normed,) = take(1)
    for index, tok in enumerate(toks):
        hat, _ = normalize_rows(tok[...].astype(F32))
        normed[part(index), :] = (hat * gain[...]).astype(BF16)
    rows = normed[...]
    for weight, out in ((w_k, k_ref), (w_v, v_ref), (w_q, q_ref)):
        out[...] = silu(nt_dot(rows, weight[...])).astype(BF16)
    gap = query_gap(ints)
    inv = floats[2 * SEQ * HEADS]
    heads = []
    for head in range(HEADS):
        query = own_q[:, cols(head)] if first else q_ref[part(0), cols(head)]
        scores = nt_dot(query, k_ref[:, cols(head)])
        weights = []
        for index in range(count):
            half = scores[:, part(index)] * (0.5 * ALPHA) + floats[(first + index) * HEADS + head]
            value = half * (jnp.tanh(half) + 1.0) * inv
            weights.append(jnp.where(gap <= ints[first + index], value, 0.0).astype(BF16))
        total = nn_dot(jnp.concatenate(weights, 1), v_ref[:, cols(head)])
        if first:
            total = total + attn_in[:, cols(head)]
        if last:
            heads.append(total)
        else:
            attn_ref[:, cols(head)] = total
    if last:
        ohat, rout = normalize_rows(jnp.concatenate(heads, 1))
        ohat_ref[...] = ohat
        gate = silu(pre_ref[...]).astype(BF16).astype(F32)
        grad = dz_ref[...] * gain_out[...] * gate
        dattn_ref[...] = norm_backward(grad, ohat, rout).astype(BF16)


def forward_step(step, scalars, toks, w_in, gain, own_q, attn, pre, dz, gain_out):
    first, count = STEPS[step]
    last = step == len(STEPS) - 1
    args = [*scalars, *toks, w_in, w_in, w_in, gain]
    specs = [SMEM, SMEM] + [VMEM] * count + [weight_spec(1), weight_spec(2), weight_spec(3), VMEM]
    rows = count * ROWS
    outs = [shape(rows, WIDTH, dtype=BF16)] * 3
    if first:
        args += [own_q, attn]
        specs += [pl.BlockSpec((ROWS, WIDTH), lambda i: (0, 0)), VMEM]
    if last:
        args += [pre, dz, gain_out]
        specs += [pl.BlockSpec((ROWS, WIDTH), lambda i: (0, 0)), VMEM, VMEM]
        outs += [shape(ROWS, WIDTH, dtype=BF16), shape(ROWS, WIDTH)]
    else:
        outs += [shape(ROWS, WIDTH)]
    return call(
        functools.partial(forward_kernel, count, first, last),
        tuple(outs),
        specs,
        scratch=[pltpu.VMEM((rows, MODEL), BF16)],
        flops=2 * rows * MODEL * 3 * WIDTH,
        moved=rows * MODEL * 2 + 3 * WIDTH * MODEL * 2,
    )(*args)


def query_kernel(*refs):
    refs = list(refs)
    take = lambda n: [refs.pop(0) for _ in range(n)]
    ints, floats = take(2)
    keys = take(len(STEPS))
    values = take(len(STEPS))
    own_q, dattn, ohat_ref, dz_ref, pre_ref, x_ref, gain_out, w_out, w_u, w_q = take(10)
    mixed_ref, send, dxh_ref = take(3)
    gap = query_gap(ints)
    inv = 0.5 * floats[2 * SEQ * HEADS]
    grads = []
    for head in range(HEADS):
        query = own_q[:, cols(head)]
        grad_out = dattn[:, cols(head)]
        total = jnp.zeros((ROWS, DH), F32)
        for (first, count), k_ref, v_ref in zip(STEPS, keys, values):
            key = k_ref[:, cols(head)]
            scores = nt_dot(query, key)
            grad_a = nt_dot(grad_out, v_ref[:, cols(head)])
            pieces = []
            for index in range(count):
                half = scores[:, part(index)] * (0.5 * ALPHA) + floats[(first + index) * HEADS + head]
                turn = jnp.tanh(half)
                slope = (1.0 + turn) * (1.0 + half * (1.0 - turn))
                value = grad_a[:, part(index)] * slope * inv
                pieces.append(jnp.where(gap <= ints[first + index], value, 0.0).astype(BF16))
            total = total + nn_dot(jnp.concatenate(pieces, 1), key)
        grads.append(total * ALPHA)
    pre_u = pre_ref[:, 0:WIDTH]
    gate = silu(pre_u).astype(BF16).astype(F32)
    scaled = ohat_ref[...] * gain_out[...]
    z = (scaled * gate).astype(BF16)
    mixed_ref[...] = (x_ref[...].astype(F32) + nn_dot(z, w_out[...])).astype(BF16)
    dpre_u = (dz_ref[...] * scaled * silu_slope(pre_u)).astype(BF16)
    dpre_q = (jnp.concatenate(grads, 1) * silu_slope(pre_ref[:, 2 * WIDTH : 3 * WIDTH])).astype(BF16)
    dxh_ref[...] = nn_dot(dpre_u, w_u[...]) + nn_dot(dpre_q, w_q[...])
    for head in range(HEADS):
        send[head, 0:ROWS, :] = dpre_u[:, cols(head)].astype(F32).T.astype(BF16)
        send[2 * HEADS + head, 0:ROWS, :] = dpre_q[:, cols(head)].astype(F32).T.astype(BF16)
        turned = z[:, cols(head)].astype(F32).T.astype(BF16)
        for quarter in range(DH // ZROWS):
            send[head * (DH // ZROWS) + quarter, ROWS:CHUNK, :] = turned[
                quarter * ZROWS : (quarter + 1) * ZROWS, :
            ]


def key_kernel(count, first, last, *refs):
    refs = list(refs)
    take = lambda n: [refs.pop(0) for _ in range(n)]
    ints, floats = take(2)
    grads = take(count)
    queries, own_k, own_v = take(3)
    if first:
        dk_in, dv_in = take(2)
    if last:
        pre_v, pre_k, early, send, dkv_ref = take(5)
        for head in range(HEADS):
            send[head] = early[head]
            send[2 * HEADS + head] = early[2 * HEADS + head]
            for late in (HEADS + head, 3 * HEADS + head):
                send[late, ROWS:CHUNK, :] = early[late, ROWS:CHUNK, :]
    else:
        dk_ref, dv_ref = take(2)
    row = lax.broadcasted_iota(jnp.int32, (ROWS, ROWS), 0)
    col = lax.broadcasted_iota(jnp.int32, (ROWS, ROWS), 1)
    gap = row - col
    live = [
        (gap <= ints[SEQ + first + index]) & (col < ints[2 * SEQ + first + index])
        for index in range(count)
    ]
    inv = floats[2 * SEQ * HEADS]
    for head in range(HEADS):
        query = queries[:, cols(head)]
        grad_rows = jnp.concatenate([ref[:, cols(head)] for ref in grads], 0)
        scores = nt_dot(own_k[:, cols(head)], query)
        grad_a = nt_dot(own_v[:, cols(head)], grad_rows)
        weights, slopes = [], []
        for index in range(count):
            half = scores[:, part(index)] * (0.5 * ALPHA) + floats[(SEQ + first + index) * HEADS + head]
            turn = jnp.tanh(half)
            above = (1.0 + turn) * inv
            weights.append(jnp.where(live[index], half * above, 0.0).astype(BF16))
            slope = grad_a[:, part(index)] * (0.5 * above) * (1.0 + half * (1.0 - turn))
            slopes.append(jnp.where(live[index], slope, 0.0).astype(BF16))
        dv = nn_dot(jnp.concatenate(weights, 1), grad_rows)
        dk = nn_dot(jnp.concatenate(slopes, 1), query)
        if first:
            dv = dv + dv_in[:, cols(head)]
            dk = dk + dk_in[:, cols(head)]
        if last:
            dv = (dv * silu_slope(pre_v[:, cols(head)])).astype(BF16)
            dk = (dk * ALPHA * silu_slope(pre_k[:, cols(head)])).astype(BF16)
            send[HEADS + head, 0:ROWS, :] = dv.astype(F32).T.astype(BF16)
            send[3 * HEADS + head, 0:ROWS, :] = dk.astype(F32).T.astype(BF16)
            dkv_ref[:, cols(head)] = dv
            dkv_ref[:, WIDTH + head * DH : WIDTH + (head + 1) * DH] = dk
        else:
            dk_ref[:, cols(head)] = dk
            dv_ref[:, cols(head)] = dv


def key_step(step, scalars, grads, queries, own_k, own_v, sums, pre, send):
    first, count = STEPS[step]
    last = step == len(STEPS) - 1
    own = pl.BlockSpec((ROWS, WIDTH), lambda i: (0, 0))
    args = [*scalars, *grads, queries, own_k, own_v]
    specs = [SMEM, SMEM] + [VMEM] * count + [VMEM, own, own]
    if first:
        args += list(sums)
        specs += [VMEM, VMEM]
    kernel = functools.partial(key_kernel, count, first, last)
    cost = dict(flops=2 * 4 * count * ROWS * ROWS * WIDTH, moved=count * ROWS * WIDTH * 4)
    if not last:
        outs = (shape(ROWS, WIDTH), shape(ROWS, WIDTH))
        return call(kernel, outs, specs, **cost)(*args)
    args += [pre, pre, send]
    specs += [
        pl.BlockSpec((ROWS, WIDTH), lambda i: (0, 1)),
        pl.BlockSpec((ROWS, WIDTH), lambda i: (0, 3)),
        VMEM,
    ]
    outs = (shape(GROUPS, CHUNK, ROWS, dtype=BF16), shape(ROWS, 2 * WIDTH, dtype=BF16))
    return call(kernel, outs, specs, **cost)(*args)


def token_kernel(x_ref, cot_ref, gain, dxh_ref, dkv, w_v, w_k, out_ref):
    hat, rstd = normalize_rows(x_ref[...].astype(F32))
    grad = dxh_ref[...] + nn_dot(dkv[:, 0:WIDTH], w_v[...]) + nn_dot(dkv[:, WIDTH:], w_k[...])
    grad = norm_backward(grad * gain[...], hat, rstd)
    out_ref[...] = (cot_ref[...].astype(F32) + grad).astype(BF16)


BATCH = 4
LANES = MODEL // 128
KEEP = 10 * LANES


def weight_kernel(me_ref, got, both, keep, give, in_sum, out_sum):
    step = pl.program_id(0)
    left = jnp.concatenate([got[g] for g in range(BATCH)], 1)
    grad_in = nn_dot(left[0:ROWS, :], jnp.concatenate([both[g, 0] for g in range(BATCH)], 0))
    grad_out = nn_dot(left[ROWS:CHUNK, :], jnp.concatenate([both[g, 1] for g in range(BATCH)], 0))

    @pl.when(step == 0)
    def _():
        in_sum[...] = grad_in
        out_sum[...] = grad_out

    @pl.when(step > 0)
    def _():
        in_sum[...] += grad_in
        out_sum[...] += grad_out

    @pl.when(step == GROUPS // BATCH - 1)
    def _():
        core = me_ref[0] & 1
        for ref, parity in ((keep, core), (give, 1 - core)):
            for chip in range(SEQ // 2):
                start = pl.multiple_of((2 * chip + parity) * 8, 8)
                rows = in_sum[pl.ds(start, 8), :]
                pair = jnp.where(
                    parity == 0,
                    out_sum[4 * chip : 4 * chip + 2, :],
                    out_sum[4 * chip + 2 : 4 * chip + 4, :],
                )
                for lane in range(LANES):
                    place = slice(lane * 128, (lane + 1) * 128)
                    ref[chip, lane * 8 : lane * 8 + 8, :] = rows[:, place]
                    low = 8 * LANES + 2 * lane
                    ref[chip, low : low + 2, :] = pair[:, place]


def weight_partials(me, got, both):
    out = shape(SEQ // 2, KEEP, 128)
    whole = pl.BlockSpec((SEQ // 2, KEEP, 128), lambda g: (0, 0, 0))
    return pl.pallas_call(
        weight_kernel,
        out_shape=(out, out),
        grid=(GROUPS // BATCH,),
        in_specs=[
            SMEM,
            pl.BlockSpec((BATCH, CHUNK, ROWS), lambda g: (g, 0, 0)),
            pl.BlockSpec((BATCH, 2, ROWS, MODEL), lambda g: (g, 0, 0, 0)),
        ],
        out_specs=(whole, whole),
        scratch_shapes=[pltpu.VMEM((ROWS, MODEL), F32), pltpu.VMEM((ZROWS, MODEL), F32)],
        compiler_params=pltpu.CompilerParams(vmem_limit_bytes=40 << 20),
        cost_estimate=pl.CostEstimate(
            flops=2 * GROUPS * ROWS * CHUNK * MODEL, bytes_accessed=9 << 20, transcendentals=0
        ),
    )(me, got, both)


def finish_kernel(parts, in_ref, out_ref):
    total = parts[0]
    for chip in range(1, SEQ // 2):
        total = total + parts[chip]
    total = total * GRAD_SCALE
    for lane in range(LANES):
        place = slice(lane * 128, (lane + 1) * 128)
        in_ref[:, place] = total[lane * 8 : lane * 8 + 8, :]
        low = 8 * LANES + 2 * lane
        out_ref[:, place] = total[low : low + 2, :]


def shifted(by):
    return [(index, (index + by) % SEQ) for index in range(SEQ)]


def hop(block, by):
    return lax.ppermute(block, "seq", shifted(by))


def across(block):
    return lax.ppermute(block, "seq", [(index, index ^ 1) for index in range(SEQ)])


def ring(block):
    arrivals = [[block, across(block)]]
    up = down = block
    for _ in range(3):
        up, down = hop(up, 2), hop(down, -2)
        arrivals.append([up, across(up), down, across(down)])
    up = hop(up, 2)
    arrivals.append([up, across(up)])
    return arrivals


def local(
    tokens,
    cotangent,
    w_in,
    w_out,
    input_norm_gain,
    gain_out,
    time_bias,
    lengths,
    assignment,
    buckets,
    block_mask,
):
    x, cot = tokens[0], cotangent[0]
    me = lax.axis_index("seq").astype(jnp.int32).reshape(1)
    gain = input_norm_gain.reshape(1, MODEL)
    gain_o = gain_out.reshape(1, WIDTH)
    own = pl.BlockSpec((ROWS, WIDTH), lambda i: (0, 0))

    arrivals = ring(x)
    scalars = make_scalars(me, lengths, assignment, buckets, block_mask, time_bias)
    pre, dz, both = call(
        own_kernel,
        (shape(ROWS, 4 * WIDTH), shape(ROWS, WIDTH), shape(2, ROWS, MODEL, dtype=BF16)),
        [VMEM] * 5,
        flops=2 * ROWS * MODEL * 5 * WIDTH,
        moved=6 << 20,
    )(x, cot, w_in, w_out, gain)
    both_all = lax.all_gather(both, "dp", axis=0, tiled=False)

    attn = own_k = own_v = own_q = None
    keys, values, queries = [], [], []
    for step in range(len(STEPS)):
        outs = forward_step(
            step, scalars, arrivals[step], w_in, gain, own_q, attn, pre, dz, gain_o
        )
        if step == 0:
            own_k, own_v, own_q = outs[:3]
        keys.append(outs[0])
        values.append(outs[1])
        queries.append(outs[2])
        if step < len(STEPS) - 1:
            attn = outs[3]
    dattn, ohat = outs[3:]

    grads = ring(dattn)
    mixed, send, dxh = call(
        query_kernel,
        (
            shape(ROWS, MODEL, dtype=BF16),
            shape(GROUPS, CHUNK, ROWS, dtype=BF16),
            shape(ROWS, MODEL),
        ),
        [SMEM, SMEM]
        + [VMEM] * (2 * len(STEPS))
        + [own, VMEM, VMEM, VMEM, VMEM, VMEM, VMEM, VMEM, weight_spec(0), weight_spec(2)],
        flops=2 * 3 * SEQ * ROWS * ROWS * WIDTH + 2 * ROWS * MODEL * 3 * WIDTH,
        moved=8 << 20,
    )(
        *scalars, *keys, *values, own_q, dattn, ohat, dz, pre, x, gain_o, w_out, w_in, w_in
    )
    sums = None
    for step in range(len(STEPS)):
        sums = key_step(
            step, scalars, grads[step], queries[step], own_k, own_v, sums, pre, send
        )
    send, dkv = sums
    got = lax.all_to_all(send, "dp", 0, 0, tiled=True)
    keep, give = weight_partials(me, got, both_all)
    total = keep + across(give)
    lanes = [[2 * chip + core for chip in range(SEQ // 2)] for core in range(2)]
    parts = lax.all_to_all(total, "seq", 0, 0, tiled=True, axis_index_groups=lanes)
    grad_in, grad_out = call(finish_kernel, (shape(8, MODEL), shape(2, MODEL)), [VMEM])(parts)

    input_gradient = call(
        token_kernel,
        shape(ROWS, MODEL, dtype=BF16),
        [VMEM] * 5 + [weight_spec(1), weight_spec(3)],
        flops=2 * ROWS * MODEL * 2 * WIDTH,
        moved=4 << 20,
    )(x, cot, gain, dxh, dkv, w_in, w_in)
    return (mixed[None], input_gradient[None], grad_in, grad_out)


def solution(mesh):
    placed = (
        P("dp", "seq", None),
        P("dp", "seq", None),
        P(),
        P(),
        P(),
        P(),
        P(),
        P("dp"),
        P("dp", None),
        P("dp", None, None),
        P("dp", None, None),
    )
    return jax.shard_map(
        local,
        mesh=mesh,
        in_specs=placed,
        out_specs=(
            P("dp", "seq", None),
            P("dp", "seq", None),
            P(("dp", "seq"), None),
            P(("dp", "seq"), None),
        ),
        check_vma=False,
    )
```

```python
import functools
import math

import jax
import jax.numpy as jnp
from jax import lax
from jax.experimental import pallas as pl
from jax.experimental.pallas import tpu as pltpu
from jax.sharding import PartitionSpec as P

EPS = 1e-05
SEQ = 16
GROUPS = 16
ROWS = 128
HEADS = 4
DH = 128
WIDTH = HEADS * DH
MODEL = 1024
ALPHA = 1.0 / math.sqrt(DH)
GRAD_SCALE = 1.0 / math.sqrt(SEQ * GROUPS * ROWS)
FAR = 1 << 20
ZROWS = WIDTH // GROUPS
CHUNK = ROWS + ZROWS
NT = (((1,), (1,)), ((), ()))
SMEM = pl.BlockSpec(memory_space=pltpu.SMEM)
VMEM = pl.BlockSpec(memory_space=pltpu.VMEM)
F32 = jnp.float32
BF16 = jnp.bfloat16

PLACES = SEQ // 2
KEY_STEPS = ((0,), (1, 2, 3, 4, 5), (6, 7))


def nt_dot(a, b):
    return lax.dot_general(a, b, NT, preferred_element_type=F32)


def nn_dot(a, b):
    return jnp.dot(a, b, preferred_element_type=F32)


def silu(values):
    half = 0.5 * values
    return half * (jnp.tanh(half) + 1.0)


def silu_slope(values):
    half = 0.5 * values
    turn = jnp.tanh(half)
    return 0.5 * (1.0 + turn) * (1.0 + half * (1.0 - turn))


def normalize_rows(values):
    mean = jnp.mean(values, -1, keepdims=True)
    centred = values - mean
    var = jnp.mean(centred * centred, -1, keepdims=True)
    rstd = lax.rsqrt(var + EPS)
    return (centred * rstd, rstd)


def norm_backward(grad_hat, hat, rstd):
    first = jnp.mean(grad_hat, -1, keepdims=True)
    second = jnp.mean(grad_hat * hat, -1, keepdims=True)
    return rstd * (grad_hat - first - hat * second)


def cols(head):
    return slice(head * DH, (head + 1) * DH)


def part(index):
    return slice(index * ROWS, (index + 1) * ROWS)


def weight(ref, index):
    return ref[index * WIDTH : (index + 1) * WIDTH, :]


def call(name, kernel, out_shape, in_specs, out_specs=None, scratch=(), busy=0, limit=24, **kw):
    if out_specs is None:
        out_specs = jax.tree.map(lambda _: VMEM, out_shape)
    return pl.pallas_call(
        kernel,
        name=name,
        out_shape=out_shape,
        in_specs=in_specs,
        out_specs=out_specs,
        scratch_shapes=list(scratch),
        compiler_params=pltpu.CompilerParams(vmem_limit_bytes=limit << 20),
        cost_estimate=pl.CostEstimate(flops=busy * 1000000000, bytes_accessed=0, transcendentals=0),
        **kw,
    )


def shape(*dims, dtype=F32):
    return jax.ShapeDtypeStruct(dims, dtype)


def slot_of(me, place):
    if place < 2:
        return me ^ place
    step, rest = divmod(place - 2, 4)
    way = (1 - 2 * (me & 1)) * (2 * (step + 1))
    base = me + SEQ + (-way if rest in (0, 2) else way)
    return (base & (SEQ - 1)) ^ (rest in (1, 2))


def scalars_kernel(me_ref, pairs, bias_ref, ints, floats):
    me = me_ref[0]
    length = pairs[1 + 2 * SEQ, 0]
    own = pairs[0, me]
    for place in range(SEQ):
        block = pairs[0, slot_of(me, place)]
        ints[place] = jnp.where(pairs[1 + SEQ + own, block] > 0, (own - block) * ROWS, -FAR)
        ints[SEQ + place] = jnp.where(pairs[1 + SEQ + block, own] > 0, (block - own) * ROWS, -FAR)
        ints[2 * SEQ + place] = length - block * ROWS
        query_bucket = pairs[1 + own, block]
        key_bucket = pairs[1 + block, own]
        for head in range(HEADS):
            floats[place * HEADS + head] = 0.5 * bias_ref[head, query_bucket]
            floats[(SEQ + place) * HEADS + head] = 0.5 * bias_ref[head, key_bucket]
    ints[3 * SEQ] = length - own * ROWS
    floats[2 * SEQ * HEADS] = 1.0 / jnp.full((), length, F32)


def make_scalars(me, lengths, assignment, buckets, block_mask, time_bias):
    length_row = jnp.broadcast_to(lengths.reshape(1, 1), (1, SEQ))
    pairs = jnp.concatenate([assignment, buckets[0], block_mask[0], length_row], 0)
    return call(
        "pair_scalars",
        scalars_kernel,
        (shape(64, dtype=jnp.int32), shape(256)),
        [SMEM] * 3,
        (SMEM, SMEM),
        busy=10,
    )(me, pairs, time_bias.T)


def query_gap(ints):
    row = lax.broadcasted_iota(jnp.int32, (ROWS, ROWS), 0)
    col = lax.broadcasted_iota(jnp.int32, (ROWS, ROWS), 1)
    return jnp.where(row < ints[3 * SEQ], col - row, FAR)


def normed_kernel(x_ref, cot_ref, gain, both_ref):
    hat, _ = normalize_rows(x_ref[...].astype(F32))
    both_ref[0] = (hat * gain[...]).astype(BF16)
    both_ref[1] = cot_ref[...]


def chip_kernel(
    both_ref, other_ref, w_in, w_out, gain, pre_ref, dz_ref, k_ref, v_ref, q_ref, normed
):
    hat, _ = normalize_rows(other_ref[...].astype(F32))
    normed[part(0), :] = both_ref[0]
    normed[part(1), :] = (hat * gain[...]).astype(BF16)
    rows = normed[...]
    pre_ref[:, 0:WIDTH] = nt_dot(normed[part(0), :], weight(w_in, 0))
    for index, out in ((1, v_ref), (2, q_ref), (3, k_ref)):
        pre = nt_dot(rows, weight(w_in, index))
        pre_ref[:, index * WIDTH : (index + 1) * WIDTH] = pre[part(0), :]
        out[...] = silu(pre).astype(BF16)
    dz_ref[...] = nt_dot(both_ref[1], w_out[...])


def chip_step(both, other, w_in, w_out, gain):
    rows = 2 * ROWS
    return call(
        "chip_rows",
        chip_kernel,
        (
            shape(ROWS, 4 * WIDTH),
            shape(ROWS, WIDTH),
            *[shape(rows, WIDTH, dtype=BF16)] * 3,
        ),
        [VMEM] * 5,
        scratch=[pltpu.VMEM((rows, MODEL), BF16)],
        busy=20,
    )(both, other, w_in, w_out, gain)


def forward_kernel(places, last, *refs):
    refs = list(refs)
    take = lambda n: [refs.pop(0) for _ in range(n)]
    ints, floats = take(2)
    toks = take(2)
    w_in, gain, own_q = take(3)
    before = None
    if len(places) > 1:
        old_k, old_v = take(2)
    else:
        (before,) = take(1)
    if last:
        pre_ref, dz_ref, gain_out = take(3)
    k_ref, v_ref, q_ref = take(3)
    if last:
        dattn_ref, ohat_ref = take(2)
    else:
        attn_ref, mark_ref = take(2)
        mark_ref[...] = jnp.zeros(MARK, F32)
    (normed,) = take(1)
    for index, tok in enumerate(toks):
        hat, _ = normalize_rows(tok[...].astype(F32))
        normed[part(index), :] = (hat * gain[...]).astype(BF16)
    rows = normed[...]
    for index, out in ((3, k_ref), (1, v_ref), (2, q_ref)):
        out[...] = silu(nt_dot(rows, weight(w_in, index))).astype(BF16)
    keys, values = [k_ref], [v_ref]
    if len(places) > 1:
        keys, values = [old_k, k_ref], [old_v, v_ref]
    blocks = [2 * place + index for place in places for index in range(2)]
    gap = query_gap(ints)
    inv = floats[2 * SEQ * HEADS]
    heads = []
    for head in range(HEADS):
        key = jnp.concatenate([ref[:, cols(head)] for ref in keys], 0)
        value = jnp.concatenate([ref[:, cols(head)] for ref in values], 0)
        scores = nt_dot(own_q[part(0), cols(head)], key)
        weights = []
        for index, block in enumerate(blocks):
            half = scores[:, part(index)] * (0.5 * ALPHA) + floats[block * HEADS + head]
            weights_now = half * (jnp.tanh(half) + 1.0) * inv
            weights.append(jnp.where(gap <= ints[block], weights_now, 0.0).astype(BF16))
        total = nn_dot(jnp.concatenate(weights, 1), value)
        if before is not None:
            total = total + before[:, cols(head)]
        if last:
            heads.append(total)
        else:
            attn_ref[:, cols(head)] = total
    if last:
        ohat, rout = normalize_rows(jnp.concatenate(heads, 1))
        ohat_ref[...] = ohat
        gate = silu(pre_ref[:, 0:WIDTH]).astype(BF16).astype(F32)
        grad = dz_ref[...] * gain_out[...] * gate
        dattn_ref[...] = norm_backward(grad, ohat, rout).astype(BF16)


def forward_step(place, scalars, toks, w_in, gain, own_q, before, pre, dz, gain_out):
    last = place == PLACES - 1
    places = (0, 1) if place == 1 else (place,)
    args = [*scalars, *toks, w_in, gain, own_q, *before]
    rows = 2 * ROWS
    outs = [shape(rows, WIDTH, dtype=BF16)] * 3
    if last:
        args += [pre, dz, gain_out]
        outs += [shape(ROWS, WIDTH, dtype=BF16), shape(ROWS, WIDTH)]
    else:
        outs += [shape(ROWS, WIDTH), shape(*MARK)]
    return call(
        f"forward_{place}",
        functools.partial(forward_kernel, places, last),
        tuple(outs),
        [SMEM, SMEM] + [VMEM] * (len(args) - 2),
        scratch=[pltpu.VMEM((rows, MODEL), BF16)],
        busy=10,
    )(*args)


def key_terms(places, ints, floats, grads, queries, own_k, own_v, dv_in, dk_in, done):
    row = lax.broadcasted_iota(jnp.int32, (ROWS, ROWS), 0)
    col = lax.broadcasted_iota(jnp.int32, (ROWS, ROWS), 1)
    gap = row - col
    blocks = [2 * place + index for place in places for index in range(2)]
    live = [(gap <= ints[SEQ + block]) & (col < ints[2 * SEQ + block]) for block in blocks]
    inv = floats[2 * SEQ * HEADS]
    for head in range(HEADS):
        query = jnp.concatenate([ref[:, cols(head)] for ref in queries], 0)
        grad_rows = jnp.concatenate([ref[:, cols(head)] for ref in grads], 0)
        scores = nt_dot(own_k[part(0), cols(head)], query)
        grad_a = nt_dot(own_v[part(0), cols(head)], grad_rows)
        weights, slopes = [], []
        for index, block in enumerate(blocks):
            half = scores[:, part(index)] * (0.5 * ALPHA) + floats[(SEQ + block) * HEADS + head]
            turn = jnp.tanh(half)
            above = (1.0 + turn) * inv
            weights.append(jnp.where(live[index], half * above, 0.0).astype(BF16))
            slope = grad_a[:, part(index)] * (0.5 * above) * (1.0 + half * (1.0 - turn))
            slopes.append(jnp.where(live[index], slope, 0.0).astype(BF16))
        dv = nn_dot(jnp.concatenate(weights, 1), grad_rows)
        dk = nn_dot(jnp.concatenate(slopes, 1), query)
        if dv_in is not None:
            dv = dv + dv_in[:, cols(head)]
            dk = dk + dk_in[:, cols(head)]
        done(head, dv, dk)


def key_kernel(places, last, *refs):
    refs = list(refs)
    take = lambda n: [refs.pop(0) for _ in range(n)]
    ints, floats = take(2)
    grads = take(2 * len(places))
    queries = take(len(places))
    own_k, own_v, dv_in, dk_in = take(4)
    if last:
        pre, early, send, dkv_ref = take(4)
        for head in range(HEADS):
            send[head] = early[head]
            send[2 * HEADS + head] = early[2 * HEADS + head]
            for late in (HEADS + head, 3 * HEADS + head):
                send[late, ROWS:CHUNK, :] = early[late, ROWS:CHUNK, :]
    else:
        dv_ref, dk_ref, mark_ref = take(3)
        mark_ref[...] = jnp.zeros(MARK, F32)

    def done(head, dv, dk):
        if not last:
            dv_ref[:, cols(head)] = dv
            dk_ref[:, cols(head)] = dk
            return
        dv = (dv * silu_slope(pre[:, cols(HEADS + head)])).astype(BF16)
        dk = (dk * ALPHA * silu_slope(pre[:, cols(3 * HEADS + head)])).astype(BF16)
        send[HEADS + head, 0:ROWS, :] = dv.astype(F32).T.astype(BF16)
        send[3 * HEADS + head, 0:ROWS, :] = dk.astype(F32).T.astype(BF16)
        dkv_ref[:, cols(head)] = dv
        dkv_ref[:, cols(HEADS + head)] = dk

    key_terms(places, ints, floats, grads, queries, own_k, own_v, dv_in, dk_in, done)


def key_step(step, scalars, grads, queries, own_k, own_v, sums, pre, send):
    places = KEY_STEPS[step]
    last = step == len(KEY_STEPS) - 1
    args = [*scalars, *[grad for place in places for grad in grads[place]]]
    args += [queries[place] for place in places]
    args += [own_k, own_v, *sums]
    if last:
        args += [pre, send]
        outs = (shape(GROUPS, CHUNK, ROWS, dtype=BF16), shape(ROWS, 2 * WIDTH, dtype=BF16))
    else:
        outs = (shape(ROWS, WIDTH), shape(ROWS, WIDTH), shape(*MARK))
    return call(
        f"key_grads_{step}",
        functools.partial(key_kernel, places, last),
        outs,
        [SMEM, SMEM] + [VMEM] * (len(args) - 2),
        busy=10,
    )(*args)


FIRST_HEADS = (0, 1)
LAST_HEADS = (2, 3)


def query_terms(heads, ints, floats, keys, values, own_q, dattn):
    gap = query_gap(ints)
    inv = 0.5 * floats[2 * SEQ * HEADS]
    grads = []
    for head in heads:
        query = own_q[part(0), cols(head)]
        grad_out = dattn[:, cols(head)]
        total = jnp.zeros((ROWS, DH), F32)
        for first in range(0, PLACES, 2):
            key = jnp.concatenate([ref[:, cols(head)] for ref in keys[first : first + 2]], 0)
            value = jnp.concatenate([ref[:, cols(head)] for ref in values[first : first + 2]], 0)
            scores = nt_dot(query, key)
            grad_a = nt_dot(grad_out, value)
            pieces = []
            for index in range(4):
                block = 2 * first + index
                half = scores[:, part(index)] * (0.5 * ALPHA) + floats[block * HEADS + head]
                turn = jnp.tanh(half)
                slope = (1.0 + turn) * (1.0 + half * (1.0 - turn))
                piece = grad_a[:, part(index)] * slope * inv
                pieces.append(jnp.where(gap <= ints[block], piece, 0.0).astype(BF16))
            total = total + nn_dot(jnp.concatenate(pieces, 1), key)
        grads.append(total * ALPHA)
    return jnp.concatenate(grads, 1)


def first_query_kernel(*refs):
    refs = list(refs)
    take = lambda n: [refs.pop(0) for _ in range(n)]
    ints, floats = take(2)
    keys = take(PLACES)
    values = take(PLACES)
    own_q, dattn, grad_other = take(3)
    dq_ref, dv_ref, dk_ref, mark_ref = take(4)
    mark_ref[...] = jnp.zeros(MARK, F32)
    dq_ref[...] = query_terms(FIRST_HEADS, ints, floats, keys, values, own_q, dattn)

    def done(head, dv, dk):
        dv_ref[:, cols(head)] = dv
        dk_ref[:, cols(head)] = dk

    key_terms(
        KEY_STEPS[0], ints, floats, [dattn, grad_other], [own_q], keys[0], values[0], None, None, done
    )


def last_query_kernel(*refs):
    refs = list(refs)
    take = lambda n: [refs.pop(0) for _ in range(n)]
    ints, floats = take(2)
    keys = take(PLACES)
    values = take(PLACES)
    own_q, dattn, first_dq, ohat_ref, dz_ref, pre_ref, x_ref, gain_out, w_out, w_in = take(10)
    mixed_ref, send, dxh_ref, mark_ref = take(4)
    mark_ref[...] = jnp.zeros(MARK, F32)
    last_dq = query_terms(LAST_HEADS, ints, floats, keys, values, own_q, dattn)
    dq = jnp.concatenate([first_dq[...], last_dq], 1)
    pre_u = pre_ref[:, 0:WIDTH]
    gate = silu(pre_u).astype(BF16).astype(F32)
    scaled = ohat_ref[...] * gain_out[...]
    z = (scaled * gate).astype(BF16)
    mixed_ref[...] = (x_ref[...].astype(F32) + nn_dot(z, w_out[...])).astype(BF16)
    dpre_u = (dz_ref[...] * scaled * silu_slope(pre_u)).astype(BF16)
    dpre_q = (dq * silu_slope(pre_ref[:, 2 * WIDTH : 3 * WIDTH])).astype(BF16)
    dxh_ref[...] = nn_dot(dpre_u, weight(w_in, 0)) + nn_dot(dpre_q, weight(w_in, 2))
    for head in range(HEADS):
        send[head, 0:ROWS, :] = dpre_u[:, cols(head)].astype(F32).T.astype(BF16)
        send[2 * HEADS + head, 0:ROWS, :] = dpre_q[:, cols(head)].astype(F32).T.astype(BF16)
        turned = z[:, cols(head)].astype(F32).T.astype(BF16)
        for quarter in range(DH // ZROWS):
            send[head * (DH // ZROWS) + quarter, ROWS:CHUNK, :] = turned[
                quarter * ZROWS : (quarter + 1) * ZROWS, :
            ]


def token_kernel(x_ref, cot_ref, gain, dxh_ref, dkv, w_in, out_ref):
    hat, rstd = normalize_rows(x_ref[...].astype(F32))
    grad = dxh_ref[...] + nn_dot(dkv[:, 0:WIDTH], weight(w_in, 1))
    grad = grad + nn_dot(dkv[:, WIDTH:], weight(w_in, 3))
    grad = norm_backward(grad * gain[...], hat, rstd)
    out_ref[...] = (cot_ref[...].astype(F32) + grad).astype(BF16)


BATCH = 2
TURNS = GROUPS // BATCH
AHEAD = 3
LANES = MODEL // 128
OWN_IN = 8
OWN_OUT = 2
FLAT = (OWN_IN + OWN_OUT) * LANES


def weight_kernel(got, both, send, held, in_sum, out_sum, flat, sems):
    copies = [
        pltpu.make_async_copy(
            both.at[pl.ds(turn * BATCH, BATCH)], held.at[pl.ds(turn * BATCH, BATCH)], sems.at[turn]
        )
        for turn in range(TURNS)
    ]
    for copy in copies[:AHEAD]:
        copy.start()
    for turn, copy in enumerate(copies):
        groups = range(turn * BATCH, (turn + 1) * BATCH)
        left = jnp.concatenate([got[g] for g in groups], 1)
        copy.wait()
        if turn + AHEAD < TURNS:
            copies[turn + AHEAD].start()
        grad_in = nn_dot(left[0:ROWS, :], jnp.concatenate([held[g, 0] for g in groups], 0))
        grad_out = nn_dot(left[ROWS:CHUNK, :], jnp.concatenate([held[g, 1] for g in groups], 0))
        if turn == 0:
            in_sum[...] = grad_in
            out_sum[...] = grad_out
        else:
            in_sum[...] += grad_in
            out_sum[...] += grad_out
    for owner in range(SEQ):
        rows = in_sum[owner * OWN_IN : (owner + 1) * OWN_IN, :]
        pair = out_sum[owner * OWN_OUT : (owner + 1) * OWN_OUT, :]
        for lane in range(LANES):
            place = slice(lane * 128, (lane + 1) * 128)
            flat[owner, lane * OWN_IN : (lane + 1) * OWN_IN, :] = rows[:, place]
            low = OWN_IN * LANES + OWN_OUT * lane
            flat[owner, low : low + OWN_OUT, :] = pair[:, place]
    send[...] = flat[...].astype(BF16)


def weight_partials(got, both):
    return call(
        "weight_partials",
        weight_kernel,
        shape(SEQ, FLAT, 128, dtype=BF16),
        [VMEM, pl.BlockSpec(memory_space=pltpu.HBM)],
        scratch=[
            pltpu.VMEM((GROUPS, 2, ROWS, MODEL), BF16),
            pltpu.VMEM((ROWS, MODEL), F32),
            pltpu.VMEM((ZROWS, MODEL), F32),
            pltpu.VMEM((SEQ, FLAT, 128), F32),
            pltpu.SemaphoreType.DMA((TURNS,)),
        ],
        busy=3,
        limit=56,
    )(got, both)


def finish_kernel(parts, in_ref, out_ref):
    total = parts[0].astype(F32)
    for owner in range(1, SEQ):
        total = total + parts[owner].astype(F32)
    total = total * GRAD_SCALE
    for lane in range(LANES):
        place = slice(lane * 128, (lane + 1) * 128)
        in_ref[:, place] = total[lane * OWN_IN : (lane + 1) * OWN_IN, :]
        low = OWN_IN * LANES + OWN_OUT * lane
        out_ref[:, place] = total[low : low + OWN_OUT, :]


def after_kernel(block, *refs):
    refs[-1][...] = block[...]


def after(block, *marks):
    out = jax.ShapeDtypeStruct(block.shape, block.dtype)
    return call("after", after_kernel, out, [VMEM] * (1 + len(marks)), limit=8)(block, *marks)


MARK = (8, 128)


def hop(block, name):
    pairs = [(index, (index + (2 if index % 2 == 0 else -2)) % SEQ) for index in range(SEQ)]
    with jax.named_scope(name):
        return lax.ppermute(block, "seq", pairs)


def across(block, name):
    with jax.named_scope(name):
        return lax.ppermute(block, "seq", [(index, index ^ 1) for index in range(SEQ)])


def local(
    tokens,
    cotangent,
    w_in,
    w_out,
    input_norm_gain,
    gain_out,
    time_bias,
    lengths,
    assignment,
    buckets,
    block_mask,
):
    x, cot = tokens[0], cotangent[0]
    me = lax.axis_index("seq").astype(jnp.int32).reshape(1)
    gain = input_norm_gain.reshape(1, MODEL)
    gain_o = gain_out.reshape(1, WIDTH)


    def forward(place, block, label, before):
        toks = [block, across(block, label)]
        outs = forward_step(place, scalars, toks, w_in, gain, own_q, before, pre, dz, gain_o)
        keys.append(outs[0])
        values.append(outs[1])
        queries.append(outs[2])
        return outs[3:4], outs[4]

    both = call("normed_rows", normed_kernel, shape(2, ROWS, MODEL, dtype=BF16), [VMEM] * 3, busy=10)(
        x, cot, gain
    )
    both_all = lax.all_gather(both, "dp", axis=0, tiled=False)
    scalars = make_scalars(me, lengths, assignment, buckets, block_mask, time_bias)

    other = across(x, "tokens_across_0")
    own_1, other_1 = hop(x, "tokens_own_1"), hop(other, "tokens_other_1")
    other_0 = after(other, own_1, other_1)
    pre, dz, own_k, own_v, own_q = chip_step(both, other_0, w_in, w_out, gain)
    keys, values, queries = [own_k], [own_v], [own_q]
    own_2, other_2 = hop(own_1, "tokens_own_2"), hop(other_1, "tokens_other_2")
    attn, mark = forward(1, own_1, "tokens_own_across_1", (own_k, own_v))
    attn, mark = forward(2, other_1, "tokens_other_across_1", attn)
    own_3 = after(hop(own_2, "tokens_own_3"), mark)
    own_4, other_3 = hop(own_3, "tokens_own_4"), hop(other_2, "tokens_other_3")
    attn, mark = forward(3, own_2, "tokens_own_across_2", attn)
    attn, mark = forward(4, other_2, "tokens_other_across_2", attn)
    other_3 = after(other_3, mark)
    attn, mark = forward(5, own_3, "tokens_own_across_3", attn)
    own_4 = after(own_4, mark)
    attn, mark = forward(6, other_3, "tokens_other_across_3", attn)
    (dattn,), ohat = forward(7, own_4, "tokens_own_across_4", attn)

    other = across(dattn, "dattn_across_0")
    own_1, other_1 = hop(dattn, "dattn_own_1"), hop(other, "dattn_other_1")
    common = [*scalars, *keys, *values, own_q]
    args = [*common, after(dattn, own_1, other_1), other]
    first_dq, dv, dk, mark = call(
        "first_query_grads",
        first_query_kernel,
        (shape(ROWS, WIDTH // 2), shape(ROWS, WIDTH), shape(ROWS, WIDTH), shape(*MARK)),
        [SMEM, SMEM] + [VMEM] * (len(args) - 2),
        busy=10,
    )(*args)
    own_2, other_2 = after(hop(own_1, "dattn_own_2"), mark), hop(other_1, "dattn_other_2")
    args = [*common, after(dattn, own_2, other_2), first_dq, ohat, dz, pre, x, gain_o, w_out, w_in]
    mixed, send, dxh, mark = call(
        "last_query_grads",
        last_query_kernel,
        (
            shape(ROWS, MODEL, dtype=BF16),
            shape(GROUPS, CHUNK, ROWS, dtype=BF16),
            shape(ROWS, MODEL),
            shape(*MARK),
        ),
        [SMEM, SMEM] + [VMEM] * (len(args) - 2),
        busy=10,
    )(*args)
    own_3, other_3 = after(hop(own_2, "dattn_own_3"), mark), hop(other_2, "dattn_other_3")
    own_4 = hop(own_3, "dattn_own_4")
    grads = {
        1: [own_1, across(own_1, "dattn_own_across_1")],
        2: [other_1, across(other_1, "dattn_other_across_1")],
        3: [own_2, across(own_2, "dattn_own_across_2")],
        4: [other_2, across(other_2, "dattn_other_across_2")],
        5: [own_3, across(own_3, "dattn_own_across_3")],
        6: [other_3, across(other_3, "dattn_other_across_3")],
    }
    grads[1][0] = after(own_1, other_3)
    *sums, mark = key_step(1, scalars, grads, queries, own_k, own_v, (dv, dk), pre, send)
    own_4 = after(own_4, mark)
    grads[7] = [own_4, across(own_4, "dattn_own_across_4")]
    send, dkv = key_step(2, scalars, grads, queries, own_k, own_v, sums, pre, send)
    got = lax.all_to_all(send, "dp", 0, 0, tiled=True)
    parts = lax.all_to_all(weight_partials(got, both_all), "seq", 0, 0, tiled=True)
    grad_in, grad_out = call(
        "weight_sums", finish_kernel, (shape(OWN_IN, MODEL), shape(OWN_OUT, MODEL)), [VMEM]
    )(parts)

    input_gradient = call(
        "token_grads",
        token_kernel, shape(ROWS, MODEL, dtype=BF16), [VMEM] * 6, busy=2
    )(x, cot, gain, dxh, dkv, w_in)
    return (mixed[None], input_gradient[None], grad_in, grad_out)


def solution(mesh):
    placed = (
        P("dp", "seq", None),
        P("dp", "seq", None),
        P(),
        P(),
        P(),
        P(),
        P(),
        P("dp"),
        P("dp", None),
        P("dp", None, None),
        P("dp", None, None),
    )
    return jax.shard_map(
        local,
        mesh=mesh,
        in_specs=placed,
        out_specs=(
            P("dp", "seq", None),
            P("dp", "seq", None),
            P(("dp", "seq"), None),
            P(("dp", "seq"), None),
        ),
        check_vma=False,
    )
```

```python
import functools
import math

import jax
import jax.numpy as jnp
from jax import lax
from jax.experimental import pallas as pl
from jax.experimental.pallas import tpu as pltpu
from jax.sharding import PartitionSpec as P

EPS = 1e-05
SEQ = 16
GROUPS = 16
ROWS = 128
HEADS = 4
DH = 128
WIDTH = HEADS * DH
MODEL = 1024
ALPHA = 1.0 / math.sqrt(DH)
GRAD_SCALE = 1.0 / math.sqrt(SEQ * GROUPS * ROWS)
FAR = 1 << 20
OWN_IN = 4 * WIDTH // (SEQ * GROUPS)
OWN_OUT = WIDTH // (SEQ * GROUPS)
LANES = MODEL // 128
NT = (((1,), (1,)), ((), ()))
SMEM = pl.BlockSpec(memory_space=pltpu.SMEM)
VMEM = pl.BlockSpec(memory_space=pltpu.VMEM)
F32 = jnp.float32
BF16 = jnp.bfloat16

PLACES = SEQ // 2
KEY_STEPS = ((0,), (1, 2, 3, 4), (5, 6, 7))


def nt_dot(a, b):
    return lax.dot_general(a, b, NT, preferred_element_type=F32)


def nn_dot(a, b):
    return jnp.dot(a, b, preferred_element_type=F32)


def silu(values):
    half = 0.5 * values
    return half * (jnp.tanh(half) + 1.0)


def silu_slope(values):
    half = 0.5 * values
    turn = jnp.tanh(half)
    return 0.5 * (1.0 + turn) * (1.0 + half * (1.0 - turn))


def normalize_rows(values):
    mean = jnp.mean(values, -1, keepdims=True)
    centred = values - mean
    var = jnp.mean(centred * centred, -1, keepdims=True)
    rstd = lax.rsqrt(var + EPS)
    return (centred * rstd, rstd)


def norm_backward(grad_hat, hat, rstd):
    first = jnp.mean(grad_hat, -1, keepdims=True)
    second = jnp.mean(grad_hat * hat, -1, keepdims=True)
    return rstd * (grad_hat - first - hat * second)


def cols(head):
    return slice(head * DH, (head + 1) * DH)


def part(index):
    return slice(index * ROWS, (index + 1) * ROWS)


def weight(ref, index):
    return ref[index * WIDTH : (index + 1) * WIDTH, :]


def call(name, kernel, out_shape, in_specs, out_specs=None, scratch=(), busy=0, limit=24, **kw):
    if out_specs is None:
        out_specs = jax.tree.map(lambda _: VMEM, out_shape)
    return pl.pallas_call(
        kernel,
        name=name,
        out_shape=out_shape,
        in_specs=in_specs,
        out_specs=out_specs,
        scratch_shapes=list(scratch),
        compiler_params=pltpu.CompilerParams(vmem_limit_bytes=limit << 20),
        cost_estimate=pl.CostEstimate(flops=busy * 1000000000, bytes_accessed=0, transcendentals=0),
        **kw,
    )


def shape(*dims, dtype=F32):
    return jax.ShapeDtypeStruct(dims, dtype)


def slot_of(me, place):
    if place < 2:
        return me ^ place
    step, rest = divmod(place - 2, 4)
    way = (1 - 2 * (me & 1)) * (2 * (step + 1))
    base = me + SEQ + (-way if rest in (0, 2) else way)
    return (base & (SEQ - 1)) ^ (rest in (1, 2))


def scalars_kernel(me_ref, pairs, bias_ref, ints, floats):
    me = me_ref[0]
    length = pairs[1 + 2 * SEQ, 0]
    own = pairs[0, me]
    for place in range(SEQ):
        block = pairs[0, slot_of(me, place)]
        ints[place] = jnp.where(pairs[1 + SEQ + own, block] > 0, (own - block) * ROWS, -FAR)
        ints[SEQ + place] = jnp.where(pairs[1 + SEQ + block, own] > 0, (block - own) * ROWS, -FAR)
        ints[2 * SEQ + place] = length - block * ROWS
        query_bucket = pairs[1 + own, block]
        key_bucket = pairs[1 + block, own]
        for head in range(HEADS):
            floats[place * HEADS + head] = 0.5 * bias_ref[head, query_bucket]
            floats[(SEQ + place) * HEADS + head] = 0.5 * bias_ref[head, key_bucket]
    ints[3 * SEQ] = length - own * ROWS
    floats[2 * SEQ * HEADS] = 1.0 / jnp.full((), length, F32)


def make_scalars(me, lengths, assignment, buckets, block_mask, time_bias):
    length_row = jnp.broadcast_to(lengths.reshape(1, 1), (1, SEQ))
    pairs = jnp.concatenate([assignment, buckets[0], block_mask[0], length_row], 0)
    return call(
        "pair_scalars",
        scalars_kernel,
        (shape(64, dtype=jnp.int32), shape(256)),
        [SMEM] * 3,
        (SMEM, SMEM),
        busy=10,
    )(me, pairs, time_bias.T)


def query_gap(ints):
    row = lax.broadcasted_iota(jnp.int32, (ROWS, ROWS), 0)
    col = lax.broadcasted_iota(jnp.int32, (ROWS, ROWS), 1)
    return jnp.where(row < ints[3 * SEQ], col - row, FAR)


def chip_kernel(
    x_ref, other_ref, cot_ref, w_in, w_out, gain, pre_ref, dz_ref, k_ref, v_ref, q_ref, normed
):
    for index, tok in enumerate((x_ref, other_ref)):
        hat, _ = normalize_rows(tok[...].astype(F32))
        normed[part(index), :] = (hat * gain[...]).astype(BF16)
    rows = normed[...]
    pre_ref[:, 0:WIDTH] = nt_dot(normed[part(0), :], weight(w_in, 0))
    for index, out in ((1, v_ref), (2, q_ref), (3, k_ref)):
        pre = nt_dot(rows, weight(w_in, index))
        pre_ref[:, index * WIDTH : (index + 1) * WIDTH] = pre[part(0), :]
        out[...] = silu(pre).astype(BF16)
    dz_ref[...] = nt_dot(cot_ref[...], w_out[...])


def chip_step(x, other, cot, w_in, w_out, gain):
    rows = 2 * ROWS
    return call(
        "chip_rows",
        chip_kernel,
        (
            shape(ROWS, 4 * WIDTH),
            shape(ROWS, WIDTH),
            *[shape(rows, WIDTH, dtype=BF16)] * 3,
            shape(rows, MODEL, dtype=BF16),
        ),
        [VMEM] * 6,
        busy=10,
    )(x, other, cot, w_in, w_out, gain)


def forward_kernel(places, last, *refs):
    refs = list(refs)
    take = lambda n: [refs.pop(0) for _ in range(n)]
    ints, floats = take(2)
    toks = take(2)
    w_in, gain, own_q = take(3)
    before = None
    if len(places) > 1:
        old_k, old_v = take(2)
    else:
        (before,) = take(1)
    if last:
        pre_ref, dz_ref, gain_out = take(3)
    k_ref, v_ref, q_ref, normed = take(4)
    if last:
        dattn_ref, ohat_ref = take(2)
    else:
        attn_ref, mark_ref = take(2)
        mark_ref[...] = jnp.zeros(MARK, F32)
    for index, tok in enumerate(toks):
        hat, _ = normalize_rows(tok[...].astype(F32))
        normed[part(index), :] = (hat * gain[...]).astype(BF16)
    rows = normed[...]
    for index, out in ((3, k_ref), (1, v_ref), (2, q_ref)):
        out[...] = silu(nt_dot(rows, weight(w_in, index))).astype(BF16)
    keys, values = [k_ref], [v_ref]
    if len(places) > 1:
        keys, values = [old_k, k_ref], [old_v, v_ref]
    blocks = [2 * place + index for place in places for index in range(2)]
    gap = query_gap(ints)
    inv = floats[2 * SEQ * HEADS]
    heads = []
    for head in range(HEADS):
        key = jnp.concatenate([ref[:, cols(head)] for ref in keys], 0)
        value = jnp.concatenate([ref[:, cols(head)] for ref in values], 0)
        scores = nt_dot(own_q[part(0), cols(head)], key)
        weights = []
        for index, block in enumerate(blocks):
            half = scores[:, part(index)] * (0.5 * ALPHA) + floats[block * HEADS + head]
            weights_now = half * (jnp.tanh(half) + 1.0) * inv
            weights.append(jnp.where(gap <= ints[block], weights_now, 0.0).astype(BF16))
        total = nn_dot(jnp.concatenate(weights, 1), value)
        if before is not None:
            total = total + before[:, cols(head)]
        if last:
            heads.append(total)
        else:
            attn_ref[:, cols(head)] = total
    if last:
        ohat, rout = normalize_rows(jnp.concatenate(heads, 1))
        ohat_ref[...] = ohat
        gate = silu(pre_ref[:, 0:WIDTH]).astype(BF16).astype(F32)
        grad = dz_ref[...] * gain_out[...] * gate
        dattn_ref[...] = norm_backward(grad, ohat, rout).astype(BF16)


def forward_step(place, last, scalars, toks, w_in, gain, own_q, before, pre, dz, gain_out):
    places = (0, 1) if place == 1 else (place,)
    args = [*scalars, *toks, w_in, gain, own_q, *before]
    rows = 2 * ROWS
    outs = [shape(rows, WIDTH, dtype=BF16)] * 3 + [shape(rows, MODEL, dtype=BF16)]
    if last:
        args += [pre, dz, gain_out]
        outs += [shape(ROWS, WIDTH, dtype=BF16), shape(ROWS, WIDTH)]
    else:
        outs += [shape(ROWS, WIDTH), shape(*MARK)]
    return call(
        f"forward_{place}",
        functools.partial(forward_kernel, places, last),
        tuple(outs),
        [SMEM, SMEM] + [VMEM] * (len(args) - 2),
        busy=10,
    )(*args)


SPREAD = HEADS * OWN_IN
CHUNK = ROWS + OWN_OUT * LANES
BLOCK_ORDER = (0, 1, 2, 3, 8, 9, 10, 11, 4, 5, 6, 7, 12, 13, 14, 15)


def spread(send, low, blocks):
    turned = [block.astype(F32).T for block in blocks]
    for owner in range(SEQ):
        rows = slice(owner * OWN_IN, (owner + 1) * OWN_IN)
        piece = jnp.concatenate([block[rows, :] for block in turned], 0)
        send[owner, low : low + SPREAD, :] = piece.astype(BF16)


def key_terms(places, ints, floats, grads, queries, own_k, own_v, dv_in, dk_in, done):
    row = lax.broadcasted_iota(jnp.int32, (ROWS, ROWS), 0)
    col = lax.broadcasted_iota(jnp.int32, (ROWS, ROWS), 1)
    gap = row - col
    blocks = [2 * place + index for place in places for index in range(2)]
    live = [(gap <= ints[SEQ + block]) & (col < ints[2 * SEQ + block]) for block in blocks]
    inv = floats[2 * SEQ * HEADS]
    for head in range(HEADS):
        query = jnp.concatenate([ref[:, cols(head)] for ref in queries], 0)
        grad_rows = jnp.concatenate([ref[:, cols(head)] for ref in grads], 0)
        scores = nt_dot(own_k[part(0), cols(head)], query)
        grad_a = nt_dot(own_v[part(0), cols(head)], grad_rows)
        weights, slopes = [], []
        for index, block in enumerate(blocks):
            half = scores[:, part(index)] * (0.5 * ALPHA) + floats[(SEQ + block) * HEADS + head]
            turn = jnp.tanh(half)
            above = (1.0 + turn) * inv
            weights.append(jnp.where(live[index], half * above, 0.0).astype(BF16))
            slope = grad_a[:, part(index)] * (0.5 * above) * (1.0 + half * (1.0 - turn))
            slopes.append(jnp.where(live[index], slope, 0.0).astype(BF16))
        dv = nn_dot(jnp.concatenate(weights, 1), grad_rows)
        dk = nn_dot(jnp.concatenate(slopes, 1), query)
        if dv_in is not None:
            dv = dv + dv_in[:, cols(head)]
            dk = dk + dk_in[:, cols(head)]
        done(head, dv, dk)


def key_kernel(places, last, *refs):
    refs = list(refs)
    take = lambda n: [refs.pop(0) for _ in range(n)]
    ints, floats = take(2)
    grads = take(2 * len(places))
    queries = take(len(places))
    own_k, own_v, dv_in, dk_in = take(4)
    if last:
        pre, part_u, part_q, part_out, send, dkv_ref = take(6)
        send[:, 0:SPREAD, :] = part_u[...]
        send[:, SPREAD : 2 * SPREAD, :] = part_q[...]
        send[:, ROWS:CHUNK, :] = part_out[...]
        made = {}
    else:
        dv_ref, dk_ref, mark_ref = take(3)
        mark_ref[...] = jnp.zeros(MARK, F32)

    def done(head, dv, dk):
        if not last:
            dv_ref[:, cols(head)] = dv
            dk_ref[:, cols(head)] = dk
            return
        dv = (dv * silu_slope(pre[:, cols(HEADS + head)])).astype(BF16)
        dk = (dk * ALPHA * silu_slope(pre[:, cols(3 * HEADS + head)])).astype(BF16)
        made[head] = (dv, dk)
        dkv_ref[:, cols(head)] = dv
        dkv_ref[:, cols(HEADS + head)] = dk

    key_terms(places, ints, floats, grads, queries, own_k, own_v, dv_in, dk_in, done)
    if last:
        spread(send, 2 * SPREAD, [made[head][0] for head in range(HEADS)])
        spread(send, 3 * SPREAD, [made[head][1] for head in range(HEADS)])


def key_step(step, scalars, grads, queries, own_k, own_v, sums, pre, parts):
    places = KEY_STEPS[step]
    last = step == len(KEY_STEPS) - 1
    args = [*scalars, *[grad for place in places for grad in grads[place]]]
    args += [queries[place] for place in places]
    args += [own_k, own_v, *sums]
    if last:
        args += [pre, *parts]
        outs = (shape(SEQ, CHUNK, ROWS, dtype=BF16), shape(ROWS, 2 * WIDTH, dtype=BF16))
    else:
        outs = (shape(ROWS, WIDTH), shape(ROWS, WIDTH), shape(*MARK))
    return call(
        f"key_grads_{step}",
        functools.partial(key_kernel, places, last),
        outs,
        [SMEM, SMEM] + [VMEM] * (len(args) - 2),
        busy=10,
    )(*args)


FIRST_HEADS = (0, 1)
LAST_HEADS = (2, 3)


def query_terms(heads, ints, floats, keys, values, own_q, dattn):
    gap = query_gap(ints)
    inv = 0.5 * floats[2 * SEQ * HEADS]
    grads = []
    for head in heads:
        query = own_q[part(0), cols(head)]
        grad_out = dattn[:, cols(head)]
        total = jnp.zeros((ROWS, DH), F32)
        for first in range(0, PLACES, 2):
            key = jnp.concatenate([ref[:, cols(head)] for ref in keys[first : first + 2]], 0)
            value = jnp.concatenate([ref[:, cols(head)] for ref in values[first : first + 2]], 0)
            scores = nt_dot(query, key)
            grad_a = nt_dot(grad_out, value)
            pieces = []
            for index in range(4):
                block = 2 * first + index
                half = scores[:, part(index)] * (0.5 * ALPHA) + floats[block * HEADS + head]
                turn = jnp.tanh(half)
                slope = (1.0 + turn) * (1.0 + half * (1.0 - turn))
                piece = grad_a[:, part(index)] * slope * inv
                pieces.append(jnp.where(gap <= ints[block], piece, 0.0).astype(BF16))
            total = total + nn_dot(jnp.concatenate(pieces, 1), key)
        grads.append(total * ALPHA)
    return jnp.concatenate(grads, 1)


def first_query_kernel(*refs):
    refs = list(refs)
    take = lambda n: [refs.pop(0) for _ in range(n)]
    ints, floats = take(2)
    keys = take(PLACES)
    values = take(PLACES)
    own_q, dattn, grad_other = take(3)
    dq_ref, dv_ref, dk_ref, mark_ref = take(4)
    mark_ref[...] = jnp.zeros(MARK, F32)
    dq_ref[...] = query_terms(FIRST_HEADS, ints, floats, keys, values, own_q, dattn)

    def done(head, dv, dk):
        dv_ref[:, cols(head)] = dv
        dk_ref[:, cols(head)] = dk

    key_terms(
        KEY_STEPS[0], ints, floats, [dattn, grad_other], [own_q], keys[0], values[0], None, None, done
    )


def last_query_kernel(*refs):
    refs = list(refs)
    take = lambda n: [refs.pop(0) for _ in range(n)]
    ints, floats = take(2)
    keys = take(PLACES)
    values = take(PLACES)
    own_q, dattn, first_dq, pre_ref, dxh_u, w_in = take(6)
    part_q, dxh_ref = take(2)
    last_dq = query_terms(LAST_HEADS, ints, floats, keys, values, own_q, dattn)
    dq = jnp.concatenate([first_dq[...], last_dq], 1)
    dpre_q = (dq * silu_slope(pre_ref[:, 2 * WIDTH : 3 * WIDTH])).astype(BF16)
    dxh_ref[...] = dxh_u[...] + nn_dot(dpre_q, weight(w_in, 2))
    spread(part_q, 0, [dpre_q[:, cols(head)] for head in range(HEADS)])


SIDE = 4


def row_kernel(
    me_ref, ohat_ref, dz_ref, pre_ref, x_ref, cot_ref, gain_out, w_out, w_in,
    mixed_ref, keep, give_1, give_2, give_3, part_u, dxh_ref, mark_ref, turned,
):
    mark_ref[...] = jnp.zeros(MARK, F32)
    pre_u = pre_ref[:, 0:WIDTH]
    gate = silu(pre_u).astype(BF16).astype(F32)
    scaled = ohat_ref[...] * gain_out[...]
    z = (scaled * gate).astype(BF16)
    for head in range(HEADS):
        turned[head] = z[:, cols(head)].astype(F32).T.astype(BF16)
    along_x = me_ref[1] // SIDE
    keep[...] = nn_dot(turned[along_x], cot_ref[...])
    for by, give in enumerate((give_1, give_2, give_3), 1):
        give[...] = nn_dot(turned[(along_x + by) & (SIDE - 1)], cot_ref[...]).astype(BF16)
    mixed_ref[...] = (x_ref[...].astype(F32) + nn_dot(z, w_out[...])).astype(BF16)
    dpre_u = (dz_ref[...] * scaled * silu_slope(pre_u)).astype(BF16)
    dxh_ref[...] = nn_dot(dpre_u, weight(w_in, 0))
    spread(part_u, 0, [dpre_u[:, cols(head)] for head in range(HEADS)])


def along_x_kernel(me_ref, own, got_1, got_2, got_3, keep, give_1, give_2, give_3, total):
    total[...] = own[...] + got_1[...].astype(F32) + got_2[...].astype(F32) + got_3[...].astype(F32)
    along_y = me_ref[1] & (SIDE - 1)
    rows = WIDTH // GROUPS
    for by, give in enumerate((keep, give_1, give_2, give_3)):
        start = pl.multiple_of(((along_y + by) & (SIDE - 1)) * rows, rows)
        give[...] = total[pl.ds(start, rows), :].astype(give.dtype)


def along_y_kernel(own, got_1, got_2, got_3, part_out):
    total = own[...] + got_1[...].astype(F32) + got_2[...].astype(F32) + got_3[...].astype(F32)
    for owner in range(SEQ):
        pair = total[owner * OWN_OUT : (owner + 1) * OWN_OUT, :]
        pieces = [pair[:, lane * 128 : (lane + 1) * 128] for lane in range(LANES)]
        part_out[owner] = jnp.concatenate(pieces, 0).astype(BF16)


def beside(block, by_x, by_y, name):
    pairs = []
    for index in range(GROUPS):
        along_x, along_y = divmod(index, SIDE)
        pairs.append((index, (along_x + by_x) % SIDE * SIDE + (along_y + by_y) % SIDE))
    with jax.named_scope(name):
        return lax.ppermute(block, "dp", pairs)


def token_kernel(x_ref, cot_ref, gain, dxh_ref, dkv, w_in, out_ref):
    hat, rstd = normalize_rows(x_ref[...].astype(F32))
    grad = dxh_ref[...] + nn_dot(dkv[:, 0:WIDTH], weight(w_in, 1))
    grad = grad + nn_dot(dkv[:, WIDTH:], weight(w_in, 3))
    grad = norm_backward(grad * gain[...], hat, rstd)
    out_ref[...] = (cot_ref[...].astype(F32) + grad).astype(BF16)


BATCH = 2


def weight_kernel(me_ref, got, *refs):
    normed, (send, out_ref, total, flat) = refs[:PLACES], refs[PLACES:]
    me = me_ref[0]
    for first in range(0, PLACES, BATCH):
        slots = [slot_of(me, place) for place in range(2 * first, 2 * (first + BATCH))]
        left = jnp.concatenate([got[slot, 0:ROWS, :] for slot in slots], 1)
        right = jnp.concatenate([normed[first + index][...] for index in range(BATCH)], 0)
        term = nn_dot(left, right)
        if first == 0:
            total[...] = term
        else:
            total[...] += term
    for index, owner in enumerate(BLOCK_ORDER):
        rows = total[index * OWN_IN : (index + 1) * OWN_IN, :]
        for lane in range(LANES):
            flat[owner, lane * OWN_IN : (lane + 1) * OWN_IN, :] = rows[:, lane * 128 : (lane + 1) * 128]
    send[...] = flat[...].astype(BF16)
    own_out = got[0, ROWS:CHUNK, :].astype(F32)
    for slot in range(1, SEQ):
        own_out = own_out + got[slot, ROWS:CHUNK, :].astype(F32)
    own_out = own_out * GRAD_SCALE
    for lane in range(LANES):
        out_ref[:, lane * 128 : (lane + 1) * 128] = own_out[lane * OWN_OUT : (lane + 1) * OWN_OUT, :]


def finish_kernel(parts, in_ref):
    total = parts[0].astype(F32)
    for group in range(1, GROUPS):
        total = total + parts[group].astype(F32)
    total = total * GRAD_SCALE
    for lane in range(LANES):
        in_ref[:, lane * 128 : (lane + 1) * 128] = total[lane * OWN_IN : (lane + 1) * OWN_IN, :]


def after_kernel(block, *refs):
    refs[-1][...] = block[...]


def after(block, *marks):
    out = jax.ShapeDtypeStruct(block.shape, block.dtype)
    return call("after", after_kernel, out, [VMEM] * (1 + len(marks)), limit=8)(block, *marks)


MARK = (8, 128)


def hop(block, name, chips=1):
    by = 2 * chips
    pairs = [(index, (index + (by if index % 2 == 0 else -by)) % SEQ) for index in range(SEQ)]
    with jax.named_scope(name):
        return lax.ppermute(block, "seq", pairs)


def across(block, name):
    with jax.named_scope(name):
        return lax.ppermute(block, "seq", [(index, index ^ 1) for index in range(SEQ)])


def local(
    tokens,
    cotangent,
    w_in,
    w_out,
    input_norm_gain,
    gain_out,
    time_bias,
    lengths,
    assignment,
    buckets,
    block_mask,
):
    x, cot = tokens[0], cotangent[0]
    me = jnp.stack([lax.axis_index("seq"), lax.axis_index("dp")]).astype(jnp.int32)
    gain = input_norm_gain.reshape(1, MODEL)
    gain_o = gain_out.reshape(1, WIDTH)


    def forward(place, block, label, before, last=False):
        toks = [block, across(block, label)]
        keys[place], values[place], queries[place], normed[place], *rest = forward_step(
            place, last, scalars, toks, w_in, gain, own_q, before, pre, dz, gain_o
        )
        return rest if last else (rest[:1], rest[1])

    scalars = make_scalars(me, lengths, assignment, buckets, block_mask, time_bias)

    other = across(x, "tokens_across_0")
    own_1, other_1 = hop(x, "tokens_own_1"), hop(other, "tokens_other_1")
    other_0 = after(other, own_1, other_1)
    pre, dz, own_k, own_v, own_q, first_normed = chip_step(x, other_0, cot, w_in, w_out, gain)
    keys, values, queries, normed = {0: own_k}, {0: own_v}, {0: own_q}, {0: first_normed}
    own_2, other_2 = hop(own_1, "tokens_own_2"), hop(other_1, "tokens_other_2")
    attn, mark = forward(1, own_1, "tokens_own_across_1", (own_k, own_v))
    attn, mark = forward(2, other_1, "tokens_other_across_1", attn)
    own_3 = after(hop(own_2, "tokens_own_3"), mark)
    own_4, other_3 = hop(own_3, "tokens_own_4"), hop(other_2, "tokens_other_3")
    attn, mark = forward(3, own_2, "tokens_own_across_2", attn)
    attn, mark = forward(4, other_2, "tokens_other_across_2", attn)
    own_4 = after(own_4, mark)
    attn, mark = forward(5, own_3, "tokens_own_across_3", attn)
    other_3 = after(other_3, mark)
    attn, mark = forward(7, own_4, "tokens_own_across_4", attn)
    dattn, ohat = forward(6, other_3, "tokens_other_across_3", attn, last=True)
    in_order = lambda held: [held[place] for place in range(PLACES)]

    other = across(dattn, "dattn_across_0")
    own_1, other_1 = hop(dattn, "dattn_own_1"), hop(other, "dattn_other_1")
    mixed, keep, *gives, part_u, dxh, mark = call(
        "row_grads",
        row_kernel,
        (
            shape(ROWS, MODEL, dtype=BF16),
            shape(DH, MODEL),
            *[shape(DH, MODEL, dtype=BF16)] * (SIDE - 1),
            shape(SEQ, SPREAD, ROWS, dtype=BF16),
            shape(ROWS, MODEL),
            shape(*MARK),
        ),
        [SMEM] + [VMEM] * 8,
        scratch=[pltpu.VMEM((HEADS, DH, ROWS), BF16)],
        busy=10,
    )(me, ohat, dz, pre, x, cot, gain_o, w_out, w_in)
    own_1 = after(own_1, mark)
    gots = [beside(give, by, 0, f"out_along_x_{by}") for by, give in enumerate(gives, 1)]
    rows = WIDTH // GROUPS
    keep, *gives = call(
        "out_along_x",
        along_x_kernel,
        (shape(rows, MODEL), *[shape(rows, MODEL, dtype=BF16)] * (SIDE - 1)),
        [SMEM] + [VMEM] * SIDE,
        scratch=[pltpu.VMEM((DH, MODEL), F32)],
        busy=3,
    )(me, keep, *gots)
    gots = [beside(give, 0, by, f"out_along_y_{by}") for by, give in enumerate(gives, 1)]
    part_out = call(
        "out_along_y",
        along_y_kernel,
        shape(SEQ, CHUNK - ROWS, 128, dtype=BF16),
        [VMEM] * SIDE,
        busy=2,
    )(keep, *gots)
    common = [*scalars, *in_order(keys), *in_order(values), own_q]
    args = [*common, after(dattn, own_1, other_1), other]
    first_dq, dv, dk, mark = call(
        "first_query_grads",
        first_query_kernel,
        (shape(ROWS, WIDTH // 2), shape(ROWS, WIDTH), shape(ROWS, WIDTH), shape(*MARK)),
        [SMEM, SMEM] + [VMEM] * (len(args) - 2),
        busy=10,
    )(*args)
    own_2, other_2 = after(hop(own_1, "dattn_own_2"), mark), hop(other_1, "dattn_other_2")
    own_3, other_3 = hop(own_2, "dattn_own_3"), hop(other_2, "dattn_other_3")
    own_4 = hop(own_2, "dattn_own_4", 2)
    args = [*common, after(dattn, own_2, other_2), first_dq, pre, dxh, w_in]
    part_q, dxh = call(
        "last_query_grads",
        last_query_kernel,
        (shape(SEQ, SPREAD, ROWS, dtype=BF16), shape(ROWS, MODEL)),
        [SMEM, SMEM] + [VMEM] * (len(args) - 2),
        busy=5,
    )(*args)
    grads = {
        1: [own_1, across(own_1, "dattn_own_across_1")],
        2: [other_1, across(other_1, "dattn_other_across_1")],
        3: [own_2, across(own_2, "dattn_own_across_2")],
        4: [other_2, across(other_2, "dattn_other_across_2")],
    }
    *sums, mark = key_step(1, scalars, grads, queries, own_k, own_v, (dv, dk), pre, None)
    own_3, other_3, own_4 = after(own_3, mark), after(other_3, mark), after(own_4, mark)
    grads[5] = [own_3, across(own_3, "dattn_own_across_3")]
    grads[6] = [other_3, across(other_3, "dattn_other_across_3")]
    grads[7] = [own_4, across(own_4, "dattn_own_across_4")]
    parts = (part_u, part_q, part_out)
    send, dkv = key_step(2, scalars, grads, queries, own_k, own_v, sums, pre, parts)

    got = lax.all_to_all(send, "seq", 0, 0, tiled=True)
    give_in, grad_out = call(
        "weight_partials",
        weight_kernel,
        (shape(GROUPS, OWN_IN * LANES, 128, dtype=BF16), shape(OWN_OUT, MODEL)),
        [SMEM] + [VMEM] * (1 + PLACES),
        scratch=[pltpu.VMEM((ROWS, MODEL), F32), pltpu.VMEM((GROUPS, OWN_IN * LANES, 128), F32)],
        busy=3,
    )(me, got, *in_order(normed))
    parts = lax.all_to_all(give_in, "dp", 0, 0, tiled=True)
    grad_in = call("weight_sums", finish_kernel, shape(OWN_IN, MODEL), [VMEM])(parts)

    input_gradient = call(
        "token_grads",
        token_kernel, shape(ROWS, MODEL, dtype=BF16), [VMEM] * 6, busy=2
    )(x, cot, gain, dxh, dkv, w_in)
    return (mixed[None], input_gradient[None], grad_in, grad_out)


def solution(mesh):
    placed = (
        P("dp", "seq", None),
        P("dp", "seq", None),
        P(),
        P(),
        P(),
        P(),
        P(),
        P("dp"),
        P("dp", None),
        P("dp", None, None),
        P("dp", None, None),
    )
    return jax.shard_map(
        local,
        mesh=mesh,
        in_specs=placed,
        out_specs=(
            P("dp", "seq", None),
            P("dp", "seq", None),
            P(("dp", "seq"), None),
            P(("dp", "seq"), None),
        ),
        check_vma=False,
    )
```

```python
import functools
import math

import jax
import jax.numpy as jnp
from jax import lax
from jax.experimental import pallas as pl
from jax.experimental.pallas import tpu as pltpu
from jax.sharding import PartitionSpec as P

EPS = 1e-05
SEQ = 16
GROUPS = 16
ROWS = 128
HEADS = 4
DH = 128
WIDTH = HEADS * DH
MODEL = 1024
ALPHA = 1.0 / math.sqrt(DH)
GRAD_SCALE = 1.0 / math.sqrt(SEQ * GROUPS * ROWS)
FAR = 1 << 20
OWN_IN = 4 * WIDTH // (SEQ * GROUPS)
OWN_OUT = WIDTH // (SEQ * GROUPS)
LANES = MODEL // 128
NT = (((1,), (1,)), ((), ()))
SMEM = pl.BlockSpec(memory_space=pltpu.SMEM)
VMEM = pl.BlockSpec(memory_space=pltpu.VMEM)
F32 = jnp.float32
BF16 = jnp.bfloat16

PLACES = SEQ // 2
KEY_STEPS = ((0,), (1, 2, 3, 4), (5, 6, 7))


def nt_dot(a, b):
    return lax.dot_general(a, b, NT, preferred_element_type=F32)


def nn_dot(a, b):
    return jnp.dot(a, b, preferred_element_type=F32)


def silu(values):
    half = 0.5 * values
    return half * (jnp.tanh(half) + 1.0)


def silu_slope(values):
    half = 0.5 * values
    turn = jnp.tanh(half)
    return 0.5 * (1.0 + turn) * (1.0 + half * (1.0 - turn))


def normalize_rows(values):
    mean = jnp.mean(values, -1, keepdims=True)
    centred = values - mean
    var = jnp.mean(centred * centred, -1, keepdims=True)
    rstd = lax.rsqrt(var + EPS)
    return (centred * rstd, rstd)


def norm_backward(grad_hat, hat, rstd):
    first = jnp.mean(grad_hat, -1, keepdims=True)
    second = jnp.mean(grad_hat * hat, -1, keepdims=True)
    return rstd * (grad_hat - first - hat * second)


def cols(head):
    return slice(head * DH, (head + 1) * DH)


def lanes(head):
    if isinstance(head, int):
        return cols(head)
    return pl.ds(pl.multiple_of(head * DH, DH), DH)


def each_head(count, body, looped=False):
    def turn(head, _):
        body(head)
        return 0

    if looped:
        lax.fori_loop(0, count, turn, 0)
    else:
        for head in range(count):
            body(head)


def part(index):
    return slice(index * ROWS, (index + 1) * ROWS)


def weight(ref, index):
    return ref[index * WIDTH : (index + 1) * WIDTH, :]


def call(name, kernel, out_shape, in_specs, out_specs=None, scratch=(), busy=0, limit=24, **kw):
    if out_specs is None:
        out_specs = jax.tree.map(lambda _: VMEM, out_shape)
    return pl.pallas_call(
        kernel,
        name=name,
        out_shape=out_shape,
        in_specs=in_specs,
        out_specs=out_specs,
        scratch_shapes=list(scratch),
        compiler_params=pltpu.CompilerParams(vmem_limit_bytes=limit << 20),
        cost_estimate=pl.CostEstimate(flops=busy * 1000000000, bytes_accessed=0, transcendentals=0),
        **kw,
    )


def shape(*dims, dtype=F32):
    return jax.ShapeDtypeStruct(dims, dtype)


def slot_of(me, place):
    if place < 2:
        return me ^ place
    step, rest = divmod(place - 2, 4)
    way = (1 - 2 * (me & 1)) * (2 * (step + 1))
    base = me + SEQ + (-way if rest in (0, 2) else way)
    return (base & (SEQ - 1)) ^ (rest in (1, 2))


def scalars_kernel(me_ref, pairs, bias_ref, ints, floats):
    me = me_ref[0]
    length = pairs[1 + 2 * SEQ, 0]
    own = pairs[0, me]
    for place in range(SEQ):
        block = pairs[0, slot_of(me, place)]
        ints[place] = jnp.where(pairs[1 + SEQ + own, block] > 0, (own - block) * ROWS, -FAR)
        ints[SEQ + place] = jnp.where(pairs[1 + SEQ + block, own] > 0, (block - own) * ROWS, -FAR)
        ints[2 * SEQ + place] = length - block * ROWS
        query_bucket = pairs[1 + own, block]
        key_bucket = pairs[1 + block, own]
        for head in range(HEADS):
            floats[place * HEADS + head] = 0.5 * bias_ref[head, query_bucket]
            floats[(SEQ + place) * HEADS + head] = 0.5 * bias_ref[head, key_bucket]
    ints[3 * SEQ] = length - own * ROWS
    floats[2 * SEQ * HEADS] = 1.0 / jnp.full((), length, F32)


def make_scalars(me, lengths, assignment, buckets, block_mask, time_bias):
    length_row = jnp.broadcast_to(lengths.reshape(1, 1), (1, SEQ))
    pairs = jnp.concatenate([assignment, buckets[0], block_mask[0], length_row], 0)
    return call(
        "pair_scalars",
        scalars_kernel,
        (shape(64, dtype=jnp.int32), shape(256)),
        [SMEM] * 3,
        (SMEM, SMEM),
        busy=10,
    )(me, pairs, time_bias.T)


def query_gap(ints):
    row = lax.broadcasted_iota(jnp.int32, (ROWS, ROWS), 0)
    col = lax.broadcasted_iota(jnp.int32, (ROWS, ROWS), 1)
    return jnp.where(row < ints[3 * SEQ], col - row, FAR)


def chip_kernel(
    x_ref, other_ref, cot_ref, w_in, w_out, gain, pre_ref, dz_ref, k_ref, v_ref, q_ref, normed
):
    for index, tok in enumerate((x_ref, other_ref)):
        hat, _ = normalize_rows(tok[...].astype(F32))
        normed[part(index), :] = (hat * gain[...]).astype(BF16)
    rows = normed[...]
    pre_ref[:, 0:WIDTH] = nt_dot(normed[part(0), :], weight(w_in, 0))
    for index, out in ((1, v_ref), (2, q_ref), (3, k_ref)):
        pre = nt_dot(rows, weight(w_in, index))
        pre_ref[:, index * WIDTH : (index + 1) * WIDTH] = pre[part(0), :]
        out[...] = silu(pre).astype(BF16)
    dz_ref[...] = nt_dot(cot_ref[...], w_out[...])


def chip_step(x, other, cot, w_in, w_out, gain):
    rows = 2 * ROWS
    return call(
        "chip_rows",
        chip_kernel,
        (
            shape(ROWS, 4 * WIDTH),
            shape(ROWS, WIDTH),
            *[shape(rows, WIDTH, dtype=BF16)] * 3,
            shape(rows, MODEL, dtype=BF16),
        ),
        [VMEM] * 6,
        busy=10,
    )(x, other, cot, w_in, w_out, gain)


def forward_kernel(places, last, *refs):
    refs = list(refs)
    take = lambda n: [refs.pop(0) for _ in range(n)]
    ints, floats = take(2)
    toks = take(2)
    w_in, gain, own_q = take(3)
    before = None
    if len(places) > 1:
        old_k, old_v = take(2)
    else:
        (before,) = take(1)
    if last:
        pre_ref, dz_ref, gain_out = take(3)
    k_ref, v_ref, q_ref, normed = take(4)
    if last:
        dattn_ref, ohat_ref = take(2)
    else:
        attn_ref, mark_ref = take(2)
        mark_ref[...] = jnp.zeros(MARK, F32)
    if last:
        (attn_ref,) = take(1)
    for index, tok in enumerate(toks):
        hat, _ = normalize_rows(tok[...].astype(F32))
        normed[part(index), :] = (hat * gain[...]).astype(BF16)
    rows = normed[...]
    for index, out in ((3, k_ref), (1, v_ref), (2, q_ref)):
        out[...] = silu(nt_dot(rows, weight(w_in, index))).astype(BF16)
    keys, values = [k_ref], [v_ref]
    if len(places) > 1:
        keys, values = [old_k, k_ref], [old_v, v_ref]
    blocks = [2 * place + index for place in places for index in range(2)]
    gap = query_gap(ints)
    inv = floats[2 * SEQ * HEADS]

    def one_head(head):
        key = jnp.concatenate([ref[:, lanes(head)] for ref in keys], 0)
        value = jnp.concatenate([ref[:, lanes(head)] for ref in values], 0)
        scores = nt_dot(own_q[part(0), lanes(head)], key)
        weights = []
        for index, block in enumerate(blocks):
            half = scores[:, part(index)] * (0.5 * ALPHA) + floats[block * HEADS + head]
            weights_now = half * (jnp.tanh(half) + 1.0) * inv
            weights.append(jnp.where(gap <= ints[block], weights_now, 0.0).astype(BF16))
        total = nn_dot(jnp.concatenate(weights, 1), value)
        if before is not None:
            total = total + before[:, lanes(head)]
        attn_ref[:, lanes(head)] = total

    each_head(HEADS, one_head)
    if last:
        ohat, rout = normalize_rows(attn_ref[...])
        ohat_ref[...] = ohat
        gate = silu(pre_ref[:, 0:WIDTH]).astype(BF16).astype(F32)
        grad = dz_ref[...] * gain_out[...] * gate
        dattn_ref[...] = norm_backward(grad, ohat, rout).astype(BF16)


def forward_step(place, last, scalars, toks, w_in, gain, own_q, before, pre, dz, gain_out):
    places = (0, 1) if place == 1 else (place,)
    args = [*scalars, *toks, w_in, gain, own_q, *before]
    rows = 2 * ROWS
    outs = [shape(rows, WIDTH, dtype=BF16)] * 3 + [shape(rows, MODEL, dtype=BF16)]
    if last:
        args += [pre, dz, gain_out]
        outs += [shape(ROWS, WIDTH, dtype=BF16), shape(ROWS, WIDTH)]
    else:
        outs += [shape(ROWS, WIDTH), shape(*MARK)]
    return call(
        f"forward_{place}",
        functools.partial(forward_kernel, places, last),
        tuple(outs),
        [SMEM, SMEM] + [VMEM] * (len(args) - 2),
        scratch=[pltpu.VMEM((ROWS, WIDTH), F32)] if last else [],
        busy=2,
    )(*args)


SPREAD = HEADS * OWN_IN
SIDE = 4
OUT_ROWS = SIDE * OWN_OUT * LANES
CHUNK = ROWS + OUT_ROWS
BLOCK_ORDER = (0, 1, 2, 3, 8, 9, 10, 11, 4, 5, 6, 7, 12, 13, 14, 15)


def spread(send, low, blocks):
    turned = [block.astype(F32).T for block in blocks]
    for owner in range(SEQ):
        rows = slice(owner * OWN_IN, (owner + 1) * OWN_IN)
        piece = jnp.concatenate([block[rows, :] for block in turned], 0)
        send[owner, low : low + SPREAD, :] = piece.astype(BF16)


def key_terms(places, ints, floats, grads, queries, own_k, own_v, dv_in, dk_in, done, looped=False):
    row = lax.broadcasted_iota(jnp.int32, (ROWS, ROWS), 0)
    col = lax.broadcasted_iota(jnp.int32, (ROWS, ROWS), 1)
    gap = row - col
    blocks = [2 * place + index for place in places for index in range(2)]
    live = [(gap <= ints[SEQ + block]) & (col < ints[2 * SEQ + block]) for block in blocks]
    inv = floats[2 * SEQ * HEADS]

    def one_head(head):
        query = jnp.concatenate([ref[:, lanes(head)] for ref in queries], 0)
        grad_rows = jnp.concatenate([ref[:, lanes(head)] for ref in grads], 0)
        scores = nt_dot(own_k[part(0), lanes(head)], query)
        grad_a = nt_dot(own_v[part(0), lanes(head)], grad_rows)
        weights, slopes = [], []
        for index, block in enumerate(blocks):
            half = scores[:, part(index)] * (0.5 * ALPHA) + floats[(SEQ + block) * HEADS + head]
            turn = jnp.tanh(half)
            above = (1.0 + turn) * inv
            weights.append(jnp.where(live[index], half * above, 0.0).astype(BF16))
            slope = grad_a[:, part(index)] * (0.5 * above) * (1.0 + half * (1.0 - turn))
            slopes.append(jnp.where(live[index], slope, 0.0).astype(BF16))
        dv = nn_dot(jnp.concatenate(weights, 1), grad_rows)
        dk = nn_dot(jnp.concatenate(slopes, 1), query)
        if dv_in is not None:
            dv = dv + dv_in[:, lanes(head)]
            dk = dk + dk_in[:, lanes(head)]
        done(head, dv, dk)

    each_head(HEADS, one_head, looped)


def key_kernel(places, last, *refs):
    refs = list(refs)
    take = lambda n: [refs.pop(0) for _ in range(n)]
    ints, floats = take(2)
    grads = take(2 * len(places))
    queries = take(len(places))
    own_k, own_v, dv_in, dk_in = take(4)
    if last:
        pre, part_u, part_q, part_out, send, dkv_ref = take(6)
        send[:, 0:SPREAD, :] = part_u[...]
        send[:, SPREAD : 2 * SPREAD, :] = part_q[...]
        send[:, ROWS:CHUNK, :] = part_out[...]
    else:
        dv_ref, dk_ref, mark_ref = take(3)
        mark_ref[...] = jnp.zeros(MARK, F32)

    def done(head, dv, dk):
        if not last:
            dv_ref[:, lanes(head)] = dv
            dk_ref[:, lanes(head)] = dk
            return
        dv = dv * silu_slope(pre[:, lanes(HEADS + head)])
        dk = dk * ALPHA * silu_slope(pre[:, lanes(3 * HEADS + head)])
        dkv_ref[:, lanes(head)] = dv.astype(BF16)
        dkv_ref[:, lanes(HEADS + head)] = dk.astype(BF16)

    key_terms(places, ints, floats, grads, queries, own_k, own_v, dv_in, dk_in, done)
    if last:
        spread(send, 2 * SPREAD, [dkv_ref[:, cols(head)] for head in range(HEADS)])
        spread(send, 3 * SPREAD, [dkv_ref[:, cols(HEADS + head)] for head in range(HEADS)])


def key_step(step, scalars, grads, queries, own_k, own_v, sums, pre, parts):
    places = KEY_STEPS[step]
    last = step == len(KEY_STEPS) - 1
    args = [*scalars, *[grad for place in places for grad in grads[place]]]
    args += [queries[place] for place in places]
    args += [own_k, own_v, *sums]
    if last:
        args += [pre, *parts]
        outs = (shape(SEQ, CHUNK, ROWS, dtype=BF16), shape(ROWS, 2 * WIDTH, dtype=BF16))
    else:
        outs = (shape(ROWS, WIDTH), shape(ROWS, WIDTH), shape(*MARK))
    return call(
        f"key_grads_{step}",
        functools.partial(key_kernel, places, last),
        outs,
        [SMEM, SMEM] + [VMEM] * (len(args) - 2),
        busy=10,
    )(*args)


HALF = HEADS // 2


def query_terms(first_head, ints, floats, keys, values, own_q, dattn, dq_ref, looped):
    gap = query_gap(ints)
    inv = 0.5 * floats[2 * SEQ * HEADS]

    def one_head(turn):
        head = first_head + turn
        query = own_q[part(0), lanes(head)]
        grad_out = dattn[:, lanes(head)]
        total = jnp.zeros((ROWS, DH), F32)
        for first in range(0, PLACES, 2):
            key = jnp.concatenate([ref[:, lanes(head)] for ref in keys[first : first + 2]], 0)
            value = jnp.concatenate([ref[:, lanes(head)] for ref in values[first : first + 2]], 0)
            scores = nt_dot(query, key)
            grad_a = nt_dot(grad_out, value)
            pieces = []
            for index in range(4):
                block = 2 * first + index
                half = scores[:, part(index)] * (0.5 * ALPHA) + floats[block * HEADS + head]
                turned = jnp.tanh(half)
                slope = (1.0 + turned) * (1.0 + half * (1.0 - turned))
                piece = grad_a[:, part(index)] * slope * inv
                pieces.append(jnp.where(gap <= ints[block], piece, 0.0).astype(BF16))
            total = total + nn_dot(jnp.concatenate(pieces, 1), key)
        dq_ref[:, lanes(turn)] = total * ALPHA

    each_head(HALF, one_head, looped)


def first_query_kernel(*refs):
    refs = list(refs)
    take = lambda n: [refs.pop(0) for _ in range(n)]
    ints, floats = take(2)
    keys = take(PLACES)
    values = take(PLACES)
    own_q, dattn, grad_other = take(3)
    dq_ref, dv_ref, dk_ref, mark_ref = take(4)
    mark_ref[...] = jnp.zeros(MARK, F32)
    query_terms(0, ints, floats, keys, values, own_q, dattn, dq_ref, True)

    def done(head, dv, dk):
        dv_ref[:, lanes(head)] = dv
        dk_ref[:, lanes(head)] = dk

    key_terms(
        KEY_STEPS[0],
        ints,
        floats,
        [dattn, grad_other],
        [own_q],
        keys[0],
        values[0],
        None,
        None,
        done,
        looped=True,
    )


def last_query_kernel(*refs):
    refs = list(refs)
    take = lambda n: [refs.pop(0) for _ in range(n)]
    ints, floats = take(2)
    keys = take(PLACES)
    values = take(PLACES)
    own_q, dattn, first_dq, pre_ref, dxh_u, w_in = take(6)
    part_q, dxh_ref, mark_ref, last_dq = take(4)
    mark_ref[...] = jnp.zeros(MARK, F32)
    query_terms(HALF, ints, floats, keys, values, own_q, dattn, last_dq, False)
    dq = jnp.concatenate([first_dq[...], last_dq[...]], 1)
    dpre_q = (dq * silu_slope(pre_ref[:, 2 * WIDTH : 3 * WIDTH])).astype(BF16)
    dxh_ref[...] = dxh_u[...] + nn_dot(dpre_q, weight(w_in, 2))
    spread(part_q, 0, [dpre_q[:, cols(head)] for head in range(HEADS)])


def row_kernel(
    me_ref, ohat_ref, dz_ref, pre_ref, x_ref, cot_ref, gain_out, w_out, w_in,
    mixed_ref, keep, give_1, give_2, give_3, part_u, dxh_ref, mark_ref, turned,
):
    mark_ref[...] = jnp.zeros(MARK, F32)
    pre_u = pre_ref[:, 0:WIDTH]
    gate = silu(pre_u).astype(BF16).astype(F32)
    scaled = ohat_ref[...] * gain_out[...]
    z = (scaled * gate).astype(BF16)
    for head in range(HEADS):
        turned[head] = z[:, cols(head)].astype(F32).T.astype(BF16)
    along_x = me_ref[1] // SIDE
    keep[...] = nn_dot(turned[along_x], cot_ref[...])
    for by, give in enumerate((give_1, give_2, give_3), 1):
        give[...] = nn_dot(turned[(along_x + by) & (SIDE - 1)], cot_ref[...]).astype(BF16)
    mixed_ref[...] = (x_ref[...].astype(F32) + nn_dot(z, w_out[...])).astype(BF16)
    dpre_u = (dz_ref[...] * scaled * silu_slope(pre_u)).astype(BF16)
    dxh_ref[...] = nn_dot(dpre_u, weight(w_in, 0))
    spread(part_u, 0, [dpre_u[:, cols(head)] for head in range(HEADS)])


def along_x_kernel(own, got_1, got_2, got_3, part_out, mark_ref, flat):
    mark_ref[...] = jnp.zeros(MARK, F32)
    total = own[...] + got_1[...].astype(F32) + got_2[...].astype(F32) + got_3[...].astype(F32)
    rows = WIDTH // GROUPS
    for owner in range(SEQ):
        for along_y in range(SIDE):
            low = along_y * rows + owner * OWN_OUT
            pair = total[low : low + OWN_OUT, :]
            for lane in range(LANES):
                place = (lane * SIDE + along_y) * OWN_OUT
                flat[owner, place : place + OWN_OUT, :] = pair[:, lane * 128 : (lane + 1) * 128]
    part_out[...] = flat[...].astype(BF16)


def beside(block, by_x, by_y, name):
    pairs = []
    for index in range(GROUPS):
        along_x, along_y = divmod(index, SIDE)
        pairs.append((index, (along_x + by_x) % SIDE * SIDE + (along_y + by_y) % SIDE))
    with jax.named_scope(name):
        return lax.ppermute(block, "dp", pairs)


def token_kernel(x_ref, cot_ref, gain, dxh_ref, dkv, w_in, out_ref):
    hat, rstd = normalize_rows(x_ref[...].astype(F32))
    grad = dxh_ref[...] + nn_dot(dkv[:, 0:WIDTH], weight(w_in, 1))
    grad = grad + nn_dot(dkv[:, WIDTH:], weight(w_in, 3))
    grad = norm_backward(grad * gain[...], hat, rstd)
    out_ref[...] = (cot_ref[...].astype(F32) + grad).astype(BF16)


BATCH = 2
FLAT = (OWN_IN + OWN_OUT) * LANES


def weight_kernel(me_ref, got, *refs):
    normed, (send, total, flat) = refs[:PLACES], refs[PLACES:]
    me = me_ref[0]
    for first in range(0, PLACES, BATCH):
        slots = [slot_of(me, place) for place in range(2 * first, 2 * (first + BATCH))]
        left = jnp.concatenate([got[slot, 0:ROWS, :] for slot in slots], 1)
        right = jnp.concatenate([normed[first + index][...] for index in range(BATCH)], 0)
        term = nn_dot(left, right)
        if first == 0:
            total[...] = term
        else:
            total[...] += term
    for index, owner in enumerate(BLOCK_ORDER):
        rows = total[index * OWN_IN : (index + 1) * OWN_IN, :]
        for lane in range(LANES):
            flat[owner, lane * OWN_IN : (lane + 1) * OWN_IN, :] = rows[:, lane * 128 : (lane + 1) * 128]
    out = got[0, ROWS:CHUNK, :].astype(F32)
    for slot in range(1, SEQ):
        out = out + got[slot, ROWS:CHUNK, :].astype(F32)
    along_x = me_ref[1] // SIDE
    for owner in range(GROUPS):
        mine = jnp.where(along_x == owner // SIDE, 1.0, 0.0)
        for lane in range(LANES):
            low = (lane * SIDE + owner % SIDE) * OWN_OUT
            place = OWN_IN * LANES + lane * OWN_OUT
            flat[owner, place : place + OWN_OUT, :] = out[low : low + OWN_OUT, :] * mine
    send[...] = flat[...].astype(BF16)


def finish_kernel(parts, in_ref, out_ref):
    total = parts[0].astype(F32)
    for group in range(1, GROUPS):
        total = total + parts[group].astype(F32)
    total = total * GRAD_SCALE
    for lane in range(LANES):
        place = slice(lane * 128, (lane + 1) * 128)
        in_ref[:, place] = total[lane * OWN_IN : (lane + 1) * OWN_IN, :]
        low = OWN_IN * LANES + lane * OWN_OUT
        out_ref[:, place] = total[low : low + OWN_OUT, :]


def after_kernel(block, *refs):
    refs[-1][...] = block[...]


def after(block, *marks):
    out = jax.ShapeDtypeStruct(block.shape, block.dtype)
    return call("after", after_kernel, out, [VMEM] * (1 + len(marks)), limit=8)(block, *marks)


MARK = (8, 128)


def hop(block, name, chips=1):
    by = 2 * chips
    pairs = [(index, (index + (by if index % 2 == 0 else -by)) % SEQ) for index in range(SEQ)]
    with jax.named_scope(name):
        return lax.ppermute(block, "seq", pairs)


def across(block, name):
    with jax.named_scope(name):
        return lax.ppermute(block, "seq", [(index, index ^ 1) for index in range(SEQ)])


def local(
    tokens,
    cotangent,
    w_in,
    w_out,
    input_norm_gain,
    gain_out,
    time_bias,
    lengths,
    assignment,
    buckets,
    block_mask,
):
    x, cot = tokens[0], cotangent[0]
    me = jnp.stack([lax.axis_index("seq"), lax.axis_index("dp")]).astype(jnp.int32)
    gain = input_norm_gain.reshape(1, MODEL)
    gain_o = gain_out.reshape(1, WIDTH)


    def forward(place, block, label, before, last=False):
        toks = [block, across(block, label)]
        keys[place], values[place], queries[place], normed[place], *rest = forward_step(
            place, last, scalars, toks, w_in, gain, own_q, before, pre, dz, gain_o
        )
        return rest if last else (rest[:1], rest[1])

    scalars = make_scalars(me, lengths, assignment, buckets, block_mask, time_bias)

    other = across(x, "tokens_across_0")
    own_1, other_1 = hop(x, "tokens_own_1"), hop(other, "tokens_other_1")
    other_0 = after(other, own_1, other_1)
    pre, dz, own_k, own_v, own_q, first_normed = chip_step(x, other_0, cot, w_in, w_out, gain)
    keys, values, queries, normed = {0: own_k}, {0: own_v}, {0: own_q}, {0: first_normed}
    own_2, other_2 = hop(own_1, "tokens_own_2"), hop(other_1, "tokens_other_2")
    attn, mark = forward(1, own_1, "tokens_own_across_1", (own_k, own_v))
    attn, mark = forward(2, other_1, "tokens_other_across_1", attn)
    own_3 = after(hop(own_2, "tokens_own_3"), mark)
    own_4, other_3 = hop(own_3, "tokens_own_4"), hop(other_2, "tokens_other_3")
    attn, mark = forward(3, own_2, "tokens_own_across_2", attn)
    attn, mark = forward(4, other_2, "tokens_other_across_2", attn)
    own_4 = after(own_4, mark)
    attn, mark = forward(5, own_3, "tokens_own_across_3", attn)
    other_3 = after(other_3, mark)
    attn, mark = forward(7, own_4, "tokens_own_across_4", attn)
    dattn, ohat = forward(6, other_3, "tokens_other_across_3", attn, last=True)
    in_order = lambda held: [held[place] for place in range(PLACES)]

    other = across(dattn, "dattn_across_0")
    own_1, other_1 = hop(dattn, "dattn_own_1"), hop(other, "dattn_other_1")
    common = [*scalars, *in_order(keys), *in_order(values), own_q]
    args = [*common, dattn, other]
    first_dq, dv, dk, mark = call(
        "first_query_grads",
        first_query_kernel,
        (shape(ROWS, WIDTH // 2), shape(ROWS, WIDTH), shape(ROWS, WIDTH), shape(*MARK)),
        [SMEM, SMEM] + [VMEM] * (len(args) - 2),
        busy=10,
    )(*args)
    mixed, keep, *gives, part_u, dxh, mark_2 = call(
        "row_grads",
        row_kernel,
        (
            shape(ROWS, MODEL, dtype=BF16),
            shape(DH, MODEL),
            *[shape(DH, MODEL, dtype=BF16)] * (SIDE - 1),
            shape(SEQ, SPREAD, ROWS, dtype=BF16),
            shape(ROWS, MODEL),
            shape(*MARK),
        ),
        [SMEM] + [VMEM] * 8,
        scratch=[pltpu.VMEM((HEADS, DH, ROWS), BF16)],
        busy=10,
    )(me, ohat, dz, pre, x, cot, gain_o, w_out, w_in)
    own_1, other_1 = after(own_1, mark, mark_2), after(other_1, mark, mark_2)
    own_2, other_2 = hop(own_1, "dattn_own_2"), hop(other_1, "dattn_other_2")
    gots = [
        beside(give, by, 0, f"out_along_x_{by}")
        for by, give in enumerate(gives, 1)
    ]
    args = [*common, dattn, first_dq, pre, dxh, w_in]
    part_q, dxh, mark = call(
        "last_query_grads",
        last_query_kernel,
        (shape(SEQ, SPREAD, ROWS, dtype=BF16), shape(ROWS, MODEL), shape(*MARK)),
        [SMEM, SMEM] + [VMEM] * (len(args) - 2),
        scratch=[pltpu.VMEM((ROWS, WIDTH // 2), F32)],
        busy=10,
    )(*args)
    own_2, other_2 = after(own_2, mark), after(other_2, mark)
    own_3, other_3 = hop(own_2, "dattn_own_3"), hop(other_2, "dattn_other_3")
    own_4 = hop(own_2, "dattn_own_4", 2)
    grads = {
        1: [own_1, across(own_1, "dattn_own_across_1")],
        2: [other_1, across(other_1, "dattn_other_across_1")],
        3: [own_2, across(own_2, "dattn_own_across_2")],
        4: [other_2, across(other_2, "dattn_other_across_2")],
    }
    part_out, mark = call(
        "out_along_x",
        along_x_kernel,
        (shape(SEQ, OUT_ROWS, 128, dtype=BF16), shape(*MARK)),
        [VMEM] * SIDE,
        scratch=[pltpu.VMEM((SEQ, OUT_ROWS, 128), F32)],
        busy=2,
    )(keep, *gots)
    grads[1][0] = after(own_1, mark)
    *sums, mark = key_step(1, scalars, grads, queries, own_k, own_v, (dv, dk), pre, None)
    other_3, own_4 = after(other_3, mark), after(own_4, mark)
    grads[5] = [own_3, across(own_3, "dattn_own_across_3")]
    grads[6] = [other_3, across(other_3, "dattn_other_across_3")]
    grads[7] = [own_4, across(own_4, "dattn_own_across_4")]
    parts = (part_u, part_q, part_out)
    send, dkv = key_step(2, scalars, grads, queries, own_k, own_v, sums, pre, parts)

    got = lax.all_to_all(send, "seq", 0, 0, tiled=True)
    give = call(
        "weight_partials",
        weight_kernel,
        shape(GROUPS, FLAT, 128, dtype=BF16),
        [SMEM] + [VMEM] * (1 + PLACES),
        scratch=[pltpu.VMEM((ROWS, MODEL), F32), pltpu.VMEM((GROUPS, FLAT, 128), F32)],
        busy=3,
    )(me, got, *in_order(normed))
    parts = lax.all_to_all(give, "dp", 0, 0, tiled=True)
    grad_in, grad_out = call(
        "weight_sums", finish_kernel, (shape(OWN_IN, MODEL), shape(OWN_OUT, MODEL)), [VMEM]
    )(parts)

    input_gradient = call(
        "token_grads",
        token_kernel, shape(ROWS, MODEL, dtype=BF16), [VMEM] * 6, busy=2
    )(x, cot, gain, dxh, dkv, w_in)
    return (mixed[None], input_gradient[None], grad_in, grad_out)


def solution(mesh):
    placed = (
        P("dp", "seq", None),
        P("dp", "seq", None),
        P(),
        P(),
        P(),
        P(),
        P(),
        P("dp"),
        P("dp", None),
        P("dp", None, None),
        P("dp", None, None),
    )
    return jax.shard_map(
        local,
        mesh=mesh,
        in_specs=placed,
        out_specs=(
            P("dp", "seq", None),
            P("dp", "seq", None),
            P(("dp", "seq"), None),
            P(("dp", "seq"), None),
        ),
        check_vma=False,
    )
```
